256 devices in a mesh: ta: 2 (over z_hi), ha: 16 (over x, z_lo), wa: 8 (over y, core).
Axes of the slice: x: 4, y: 4, z: 8 (z_hi: 2, z_lo: 4; z = z_hi * 4 + z_lo), core: 2. Of those that a mesh axis runs over, the one named last changes fastest.
Arguments:
- queries: bfloat16 [4, 64, 128, 1536], P('ta', 'ha', 'wa'), may hold values from -5 to 5
- keys: bfloat16 [4, 64, 128, 1536], P('ta', 'ha', 'wa'), may hold values from -5 to 5
- values: bfloat16 [4, 64, 128, 1536], P('ta', 'ha', 'wa'), may hold values from -6 to 6
- out_grad: bfloat16 [4, 64, 128, 1536], P('ta', 'ha', 'wa'), may hold values from -6 to 6
- head_window: int32 [12, 3], replicated, may hold values from 0 to 1, as said below
Outputs:
- attended: bfloat16 [4, 64, 128, 1536], P('ta', 'ha', 'wa')
- query_grad: bfloat16 [4, 64, 128, 1536], P('ta', 'ha', 'wa')
- key_grad: bfloat16 [4, 64, 128, 1536], P('ta', 'ha', 'wa')
- value_grad: bfloat16 [4, 64, 128, 1536], P('ta', 'ha', 'wa')
The draws below stay inside these ranges and needn't reach their ends.
Inputs may be any that keep to these rules, and one draw needn't show every extreme that they name: `head_window`: at least one head has radius 1 along all three dimensions, and at least one radius is 0.
All inputs are finite; a program needn't handle non-finite values.
Results may differ from the reference program's by a relative error of at most 0.012.
The reference program's roundings to bfloat16 on the way (of `weights` and `dscores`) count: a program that leaves them out, or rounds other values in their place, can miss the bound.
Values may be sent and summed in bfloat16 or wider, within the bound.
No kernel may reach another device: no remote copies, remote signals or barrier semaphores. Data moves between devices by JAX's collectives and lax.ppermute only.
A program may use at most 128 MiB of HBM per device.

```python
import math
from functools import partial
import jax
import jax.numpy as jnp
from jax import lax

HEADS = 12
HEAD_DIM = 128
TILE = 2
TB = 2
HB = 4
WB = 16
NT = 4
NH = 64
NW = 128
N_TA = 2
N_HA = 16
N_WA = 8


def draw_queries(key, part):
    key = jax.random.fold_in(key, 1)
    return jnp.clip(jax.random.normal(key, (NT, NH, NW, HEADS * HEAD_DIM), jnp.float32), -4.0, 4.0).astype(jnp.bfloat16)


def draw_keys(key, part):
    key = jax.random.fold_in(key, 2)
    return jnp.clip(jax.random.normal(key, (NT, NH, NW, HEADS * HEAD_DIM), jnp.float32), -4.0, 4.0).astype(jnp.bfloat16)


def draw_head_window(key, part):
    key = jax.random.fold_in(key, 3)
    key_radii, key_full, key_axis = jax.random.split(key, 3)
    radii = jax.random.randint(key_radii, (HEADS, 3), 0, 2)
    full_head = jax.random.randint(key_full, (), 0, HEADS)
    narrow_axis = jax.random.randint(key_axis, (), 0, 3)
    head_ids = jnp.arange(HEADS)[:, None]
    axis_ids = jnp.arange(3)[None, :]
    narrow = (head_ids == (full_head + 1) % HEADS) & (axis_ids == narrow_axis)
    radii = jnp.where(narrow, 0, radii)
    return jnp.where(head_ids == full_head, 1, radii).astype(jnp.int32)


def steps_of(rng, shape, cuts, least, largest):
    def one(axis_at, shards_of):
        draws = jax.random.uniform(jax.random.fold_in(jax.random.fold_in(rng, 6), axis_at), (shards_of,), jnp.float32, least / len(cuts), largest / len(cuts))
        return jnp.repeat(jnp.exp(draws), shape[axis_at] // shards_of).reshape((-1,) + (1,) * (len(shape) - axis_at - 1))

    factor_of = one(*cuts[0])
    for cut in cuts[1:]:
        factor_of = factor_of * one(*cut)
    return factor_of


def bell_draw(own_key, dims, deviation, most, cuts=(), kind=jnp.bfloat16):
    level = steps_of(own_key, dims, cuts, -0.22, 0.18) if cuts else 1.0
    result = jax.random.normal(own_key, dims, jnp.float32) * deviation * level
    return jnp.minimum(jnp.maximum(result, -most), most).astype(kind)


def setup_inputs(seed: int = 0) -> dict:
    streams_of = jax.random.split(jax.random.key(seed), 6)
    queries = draw_queries(jax.random.fold_in(streams_of[5], 71), 0)
    keys = draw_keys(jax.random.fold_in(streams_of[5], 71), 0)
    values = bell_draw(streams_of[2], (NT, NH, NW, HEADS * HEAD_DIM), 1.0, 6.0, ((0, 2), (1, 16), (2, 8)))
    out_grad = bell_draw(streams_of[3], (NT, NH, NW, HEADS * HEAD_DIM), 1.0, 6.0, ((0, 2), (1, 16), (2, 8)))
    head_window = draw_head_window(jax.random.fold_in(streams_of[5], 71), 0)
    return {"queries": queries, "keys": keys, "values": values, "out_grad": out_grad, "head_window": head_window}


NEG_FILL = -1e+30

def axis_allow(radius, pos_a, pos_b, grid_size):
    near = jnp.abs(pos_a[:, None] // TILE - pos_b[None, :] // TILE)
    inside_a = (pos_a >= 0) & (pos_a < grid_size)
    inside_b = (pos_b >= 0) & (pos_b < grid_size)
    return (near[None, :, :] <= radius[:, None, None]) & inside_a[None, :, None] & inside_b[None, None, :]

def window_mask(window, starts_a, sizes_a, starts_b, sizes_b, limits):
    planes = []
    for dim_index in range(3):
        pos_a = starts_a[dim_index] + jnp.arange(sizes_a[dim_index], dtype=jnp.int32)
        pos_b = starts_b[dim_index] + jnp.arange(sizes_b[dim_index], dtype=jnp.int32)
        planes.append(axis_allow(window[:, dim_index], pos_a, pos_b, limits[dim_index]))
    joined = planes[0][:, :, None, None, :, None, None] & planes[1][:, None, :, None, None, :, None] & planes[2][:, None, None, :, None, None, :]
    count_a = sizes_a[0] * sizes_a[1] * sizes_a[2]
    count_b = sizes_b[0] * sizes_b[1] * sizes_b[2]
    return joined.reshape(window.shape[0], count_a, count_b)

def split_heads(tensor, head_count):
    rows = tensor.shape[0] * tensor.shape[1] * tensor.shape[2]
    return tensor.reshape(rows, head_count, -1).transpose(1, 0, 2)

def merge_heads(tensor, sizes):
    return tensor.transpose(1, 0, 2).reshape(sizes[0], sizes[1], sizes[2], -1)

def query_head(pieces, score_scale):
    query, key_rows, value_rows, grad_rows, allowed = pieces
    scores = jnp.dot(query, key_rows.T, preferred_element_type=jnp.float32) * score_scale
    scores = jnp.where(allowed, scores, NEG_FILL)
    row_max = lax.optimization_barrier(jnp.max(scores, axis=1, keepdims=True))
    log_total = row_max + jnp.log(lax.optimization_barrier(jnp.sum(jnp.exp(scores - row_max), axis=1, keepdims=True)))
    probs = jnp.exp(scores - log_total)
    weights = probs.astype(jnp.bfloat16)
    attended = jnp.dot(weights, value_rows, preferred_element_type=jnp.float32).astype(jnp.bfloat16)
    delta = lax.optimization_barrier(jnp.sum(grad_rows.astype(jnp.float32) * attended.astype(jnp.float32), axis=1))
    dprobs = jnp.dot(grad_rows, value_rows.T, preferred_element_type=jnp.float32)
    dscores = (probs * (dprobs - delta[:, None])).astype(jnp.bfloat16)
    query_grad = (jnp.dot(dscores, key_rows, preferred_element_type=jnp.float32) * score_scale).astype(jnp.bfloat16)
    return (attended, query_grad, log_total[:, 0], delta)

def key_head(pieces, score_scale):
    query, grad_rows, log_total, delta, key_rows, value_rows, allowed = pieces
    scores = jnp.dot(query, key_rows.T, preferred_element_type=jnp.float32) * score_scale
    scores = jnp.where(allowed, scores, NEG_FILL)
    probs = jnp.exp(scores - log_total[:, None])
    weights = probs.astype(jnp.bfloat16)
    dprobs = jnp.dot(grad_rows, value_rows.T, preferred_element_type=jnp.float32)
    dscores = (probs * (dprobs - delta[:, None])).astype(jnp.bfloat16)
    key_part = jnp.dot(dscores.T, query, preferred_element_type=jnp.float32) * score_scale
    value_part = jnp.dot(weights.T, grad_rows, preferred_element_type=jnp.float32)
    return (key_part, value_part)

def to_grid(boxed):
    channels = boxed.shape[-1]
    shaped = boxed.reshape(N_TA, N_HA, N_WA, TB, HB, WB, channels)
    return shaped.transpose(0, 3, 1, 4, 2, 5, 6).reshape(NT, NH, NW, channels)

def reference(queries, keys, values, out_grad, head_window):
    features = HEADS * HEAD_DIM
    score_scale = 1.0 / math.sqrt(HEAD_DIM)
    limits = (NT, NH, NW)
    own_sizes = (TB, HB, WB)
    grown_sizes = (TB + 2 * TILE, HB + 2 * TILE, WB + 2 * TILE)
    padding = ((TILE, TILE), (TILE, TILE), (TILE, TILE), (0, 0))
    padded_kv = jnp.pad(jnp.concatenate([keys, values], axis=3), padding)
    box_ids = jnp.arange(N_TA * N_HA * N_WA, dtype=jnp.int32)
    zero_index = jnp.zeros((), jnp.int32)

    def corner(box_id):
        return (box_id // (N_HA * N_WA) * TB, box_id // N_WA % N_HA * HB, box_id % N_WA * WB)

    def query_box(box_id):
        anchor = corner(box_id)
        outer_start = tuple((start - TILE for start in anchor))
        allowed = window_mask(head_window, anchor, own_sizes, outer_start, grown_sizes, limits)
        own_query = lax.dynamic_slice(queries, anchor + (zero_index,), own_sizes + (features,))
        own_grad = lax.dynamic_slice(out_grad, anchor + (zero_index,), own_sizes + (features,))
        grown_kv = lax.dynamic_slice(padded_kv, anchor + (zero_index,), grown_sizes + (2 * features,))
        pieces = (split_heads(own_query, HEADS), split_heads(grown_kv[..., :features], HEADS), split_heads(grown_kv[..., features:], HEADS), split_heads(own_grad, HEADS), allowed)
        attended, query_grad, log_total, delta = lax.map(partial(query_head, score_scale=score_scale), pieces)
        row_stats = jnp.concatenate([log_total.T.reshape(TB, HB, WB, HEADS), delta.T.reshape(TB, HB, WB, HEADS)], axis=3)
        return (merge_heads(attended, own_sizes), merge_heads(query_grad, own_sizes), row_stats)
    attended_boxes, query_boxes, stat_boxes = lax.map(query_box, box_ids)
    attended = to_grid(attended_boxes)
    query_grad = to_grid(query_boxes)
    padded_stats = jnp.pad(to_grid(stat_boxes), padding)
    padded_qg = jnp.pad(jnp.concatenate([queries, out_grad], axis=3), padding)

    def key_box(box_id):
        anchor = corner(box_id)
        outer_start = tuple((start - TILE for start in anchor))
        allowed = window_mask(head_window, anchor, own_sizes, outer_start, grown_sizes, limits)
        own_keys = lax.dynamic_slice(keys, anchor + (zero_index,), own_sizes + (features,))
        own_values = lax.dynamic_slice(values, anchor + (zero_index,), own_sizes + (features,))
        far_qg = lax.dynamic_slice(padded_qg, anchor + (zero_index,), grown_sizes + (2 * features,))
        far_stats = lax.dynamic_slice(padded_stats, anchor + (zero_index,), grown_sizes + (2 * HEADS,))
        far_total = far_stats[..., :HEADS].reshape(-1, HEADS).T
        far_delta = far_stats[..., HEADS:].reshape(-1, HEADS).T
        pieces = (split_heads(far_qg[..., :features], HEADS), split_heads(far_qg[..., features:], HEADS), far_total, far_delta, split_heads(own_keys, HEADS), split_heads(own_values, HEADS), allowed.transpose(0, 2, 1))
        key_part, value_part = lax.map(partial(key_head, score_scale=score_scale), pieces)
        return (merge_heads(key_part, own_sizes).astype(jnp.bfloat16), merge_heads(value_part, own_sizes).astype(jnp.bfloat16))
    key_boxes, value_boxes = lax.map(key_box, box_ids)
    return (attended, query_grad, to_grid(key_boxes), to_grid(value_boxes))
```

```python
from functools import partial
import math

import jax
import jax.numpy as jnp
from jax import lax
from jax.experimental import pallas as pl
from jax.experimental.pallas import tpu as pltpu
from jax.sharding import PartitionSpec as P

NEG = -1e30
BF = jnp.bfloat16
F32 = jnp.float32

GROUPS = 4
LANES = 384
HEAD = 128
GH = LANES // HEAD
TAH = ("ta", "ha")


def place():
    ta, ha = lax.axis_index("ta"), lax.axis_index("ha")
    x, z_lo = ha // 4, ha % 4
    z = ta * 4 + z_lo
    src = ta * 2 + z_lo % 2
    group = z // 2
    half = (z + x) % 2
    return src, group, half, x


def lin(x, z):
    return (z // 4) * 16 + x * 4 + z % 4


def deal_pairs(turn, back):
    pairs = []
    for x in range(4):
        for z in range(8):
            src = (z // 4) * 2 + z % 2
            dest = 2 * (src ^ turn) + ((z % 4) // 2 + x) % 2
            pair = (lin(x, z), lin(x, dest))
            pairs.append(pair[::-1] if back else pair)
    return pairs


def deal(bufs, back):
    return [lax.ppermute(b, TAH, deal_pairs(r, back)) for r, b in enumerate(bufs)]


PARTNER = [(lin(x, z), lin(x, z ^ 1)) for x in range(4) for z in range(8)]


def across_pairs():
    pairs = []
    for x in range(4):
        for z in range(8):
            other = x + 1 if (z + x) % 2 else x - 1
            if 0 <= other < 4:
                pairs.append((lin(x, z), lin(other, z)))
    return pairs


def rows_swap(partner_buf, across_buf):
    return (
        lax.ppermute(partner_buf, TAH, PARTNER),
        lax.ppermute(across_buf, TAH, across_pairs()),
    )


def cols_swap(first, last):
    n = lax.axis_size("wa")
    from_next = lax.ppermute(first, "wa", [(i + 1, i) for i in range(n - 1)])
    from_prev = lax.ppermute(last, "wa", [(i, i + 1) for i in range(n - 1)])
    return from_prev, from_next


def call(body, outs, scratch=(), grid=None, in_specs=None, out_specs=None, flops=0, size=3 << 20, name=None):
    kw = {}
    if grid is not None:
        kw = dict(grid=grid, in_specs=in_specs, out_specs=out_specs)
    return pl.pallas_call(
        body,
        out_shape=outs,
        scratch_shapes=list(scratch),
        compiler_params=pltpu.CompilerParams(vmem_limit_bytes=48 << 20),
        cost_estimate=pl.CostEstimate(flops=flops, bytes_accessed=size, transcendentals=0),
        name=name,
        **kw,
    )


def shaped(*dims, dtype=BF):
    return jax.ShapeDtypeStruct(dims, dtype)


DEALT = (2, 4, 2, 16, LANES)


def pack_body(a_ref, b_ref, *outs):
    src, _, _, _ = place()
    for r, out in enumerate(outs):
        lanes = pl.ds(pl.multiple_of((src ^ r) * LANES, LANES), LANES)
        for i, ref in enumerate((a_ref, b_ref)):
            for t in range(2):
                for h in range(4):
                    out[i, h, t] = ref[t, h, :, lanes]


def pack(a, b, name):
    return call(pack_body, [shaped(*DEALT)] * GROUPS, name=name)(a, b)


def unpack_body(*refs):
    bufs, outs = refs[:GROUPS], refs[GROUPS:]
    src, _, _, _ = place()
    for r, buf in enumerate(bufs):
        lanes = pl.ds(pl.multiple_of((src ^ r) * LANES, LANES), LANES)
        for i, ref in enumerate(outs):
            for t in range(2):
                for h in range(4):
                    ref[t, h, :, lanes] = buf[i, h, t]


def unpack(bufs, name):
    return call(unpack_body, [shaped(2, 4, 16, GROUPS * LANES)] * 2, name=name)(*bufs)


def spot(src, h):
    return pl.multiple_of((src % 2) * 256 + h * 64 + (src // 2) * 32, 32)


def gather_blocks(bufs, i, store):
    _, group, _, _ = place()
    for r, buf in enumerate(bufs):
        src = group ^ r
        for h in range(4):
            store(pl.ds(spot(src, h), 32), buf[i, h].reshape(32, buf.shape[-1]))


def edge_pick(transpose):
    shape = (512, 128) if transpose else (128, 512)
    e = lax.broadcasted_iota(jnp.int32, shape, 1 if transpose else 0)
    token = lax.broadcasted_iota(jnp.int32, shape, 0 if transpose else 1)
    want = (e % 64) // 2 * 16 + e % 2 + 14 * (e // 64)
    return jnp.where(token == want, 1.0, 0.0).astype(BF)


def own_body(*refs):
    bufs, (own, first, last) = refs[:GROUPS], refs[GROUPS:]
    pick = edge_pick(False)
    for i in range(2):
        def store(at, value, i=i):
            own[i, at, :] = value
        gather_blocks(bufs, i, store)
        edges = jnp.dot(pick, own[i], preferred_element_type=F32).astype(BF)
        first[i] = edges[:64]
        last[i] = edges[64:]


def own_kv(bufs):
    outs = [shaped(2, 512, LANES), shaped(2, 64, LANES), shaped(2, 64, LANES)]
    return call(own_body, outs, name="own_kv")(*bufs)


def rows_body(own, left, right, to_partner, to_across):
    _, _, half, _ = place()
    for out, low in ((to_partner, half), (to_across, 1 - half)):
        at = pl.multiple_of((1 - low) * 384, 128)
        side = pl.multiple_of((1 - low) * 48, 16)
        out[:, 0:128] = own[:, pl.ds(at, 128)]
        out[:, 128:144] = left[:, pl.ds(side, 16)]
        out[:, 144:160] = right[:, pl.ds(side, 16)]


def rows_out(own, left, right):
    return call(rows_body, [shaped(2, 160, LANES)] * 2, name="rows_out")(own, left, right)


def attend_body(window, own, left, right, partner, across, *refs):
    qd = refs[:GROUPS]
    back = refs[GROUPS : 2 * GROUPS]
    own_grad, side_grad, to_partner, to_across = refs[2 * GROUPS : 2 * GROUPS + 4]
    kv_mid, kv_left, kv_right, g_mid, g_left, g_right, q_all, o_all = refs[2 * GROUPS + 4 :]
    _, group, half, x = place()
    w_at = lax.axis_index("wa")
    w_last = lax.axis_size("wa") - 1
    scale = 1.0 / math.sqrt(HEAD)
    head = group * GH + pl.program_id(0)
    rad_t, rad_h, rad_w = window[head, 0], window[head, 1], window[head, 2]

    spots = []
    for buf, low in ((partner, half), (across, 1 - half)):
        at = pl.multiple_of((1 - low) * 640, 128)
        side = pl.multiple_of((1 - low) * 80, 16)
        spots.append((buf, at, side))
    for i in range(2):
        kv_mid[i, 128:640] = own[i]
        kv_left[i, 16:80] = left[i]
        kv_right[i, 16:80] = right[i]
        for buf, at, side in spots:
            kv_mid[i, pl.ds(at, 128)] = buf[i, 0:128]
            kv_left[i, pl.ds(side, 16)] = buf[i, 128:144]
            kv_right[i, pl.ds(side, 16)] = buf[i, 144:160]

        def store(at, value, i=i):
            q_all[i, at, :] = value
        gather_blocks(qd, i, store)
    g_mid[...] = jnp.zeros_like(g_mid)
    g_left[...] = jnp.zeros_like(g_left)
    g_right[...] = jnp.zeros_like(g_right)

    qi = lax.broadcasted_iota(jnp.int32, (128, 1), 0)
    q_t, q_w = qi // 32 % 2, qi % 16 // 2
    ki = lax.broadcasted_iota(jnp.int32, (1, 480), 1)
    mid = ki < 384
    ks = jnp.where(ki < 432, ki - 384, ki - 432)
    k_t = jnp.where(mid, ki // 32 % 2, ks // 4 % 2)
    k_w = jnp.where(mid, ki % 16 // 2, jnp.where(ki < 432, -1, 8))
    k_h = jnp.where(mid, ki // 128, ks // 16)
    near = (jnp.abs(q_t - k_t) <= rad_t) & (jnp.abs(q_w - k_w) <= rad_w)
    base = jnp.where(near, 0.0, NEG)
    inside = ((k_w >= 0) | (w_at > 0)) & ((k_w < 8) | (w_at < w_last))
    inside = inside & (jnp.abs(k_h - 1) <= rad_h)
    tile_row = (x * 2 + half) * 4 - 1
    tile_rows = 4 * 8

    for blk in range(4):
        row = tile_row + blk + k_h
        row_bias = jnp.where(inside & (row >= 0) & (row < tile_rows), 0.0, NEG)
        mid_at, side_at, q_at = pl.ds(128 * blk, 384), pl.ds(16 * blk, 48), pl.ds(128 * blk, 128)
        k, v = (
            jnp.concatenate([kv_mid[i, mid_at], kv_left[i, side_at], kv_right[i, side_at]], axis=0)
            for i in range(2)
        )
        q, do = q_all[0, q_at], q_all[1, q_at]
        nt = (((1,), (1,)), ((), ()))
        tn = (((0,), (0,)), ((), ()))
        s = lax.dot_general(q, k, nt, preferred_element_type=F32) * scale + (base + row_bias)
        top = jnp.max(s, axis=1, keepdims=True)
        e = jnp.exp(s - top)
        p = e * (1.0 / jnp.sum(e, axis=1, keepdims=True))
        wts = p.astype(BF)
        o = jnp.dot(wts, v, preferred_element_type=F32).astype(BF)
        delta = jnp.sum(do.astype(F32) * o.astype(F32), axis=1, keepdims=True)
        dp = lax.dot_general(do, v, nt, preferred_element_type=F32)
        ds = (p * (dp - delta)).astype(BF)
        dq = jnp.dot(ds, k, preferred_element_type=F32) * scale
        o_all[0, q_at] = o
        o_all[1, q_at] = dq.astype(BF)
        dk = lax.dot_general(ds, q, tn, preferred_element_type=F32) * scale
        dv = lax.dot_general(wts, do, tn, preferred_element_type=F32)
        for i, d in enumerate((dk, dv)):
            g_mid[i, mid_at] += d[0:384]
            g_left[i, side_at] += d[384:432]
            g_right[i, side_at] += d[432:480]

    for r, out in enumerate(back):
        src = group ^ r
        for i in range(2):
            for h in range(4):
                out[i, h] = o_all[i, pl.ds(spot(src, h), 32), :].reshape(2, 16, HEAD)
    for i in range(2):
        own_grad[i] = g_mid[i, 128:640]
        side_grad[i, 0:64] = g_left[i, 16:80]
        side_grad[i, 64:128] = g_right[i, 16:80]
        for out, (_, at, side) in zip((to_partner, to_across), spots):
            out[i, 0:128] = g_mid[i, pl.ds(at, 128)].astype(BF)
            out[i, 128:144] = g_left[i, pl.ds(side, 16)].astype(BF)
            out[i, 144:160] = g_right[i, pl.ds(side, 16)].astype(BF)


def by_head(*dims):
    lead = len(dims) - 1
    return pl.BlockSpec(dims[:-1] + (HEAD,), lambda n: (0,) * lead + (n,))


def attend(window, own, left, right, partner, across, qd):
    outs = [shaped(*DEALT)] * GROUPS + [
        shaped(2, 512, LANES, dtype=F32),
        shaped(2, 128, LANES, dtype=F32),
        shaped(2, 160, LANES),
        shaped(2, 160, LANES),
    ]
    ins = [own, left, right, partner, across] + list(qd)
    scratch = [
        pltpu.VMEM((2, 768, HEAD), BF),
        pltpu.VMEM((2, 96, HEAD), BF),
        pltpu.VMEM((2, 96, HEAD), BF),
        pltpu.VMEM((2, 768, HEAD), F32),
        pltpu.VMEM((2, 96, HEAD), F32),
        pltpu.VMEM((2, 96, HEAD), F32),
        pltpu.VMEM((2, 512, HEAD), BF),
        pltpu.VMEM((2, 512, HEAD), BF),
    ]
    return call(
        attend_body,
        outs,
        scratch,
        grid=(GH,),
        in_specs=[pl.BlockSpec(memory_space=pltpu.SMEM)] + [by_head(*a.shape) for a in ins],
        out_specs=[by_head(*a.shape) for a in outs],
        flops=1200000000,
        size=8 << 20,
        name="attend",
    )(window, *ins)


def side_body(side_grad, partner, across, to_prev, to_next):
    _, _, half, _ = place()
    for i in range(2):
        for out, lo, first in ((to_prev, 0, 128), (to_next, 64, 144)):
            out[i] = side_grad[i, lo : lo + 64].astype(BF)
            for buf, low in ((partner, half), (across, 1 - half)):
                at = pl.multiple_of((1 - low) * 48, 16)
                total = side_grad[i, pl.ds(lo + at, 16)] + buf[i, first : first + 16].astype(F32)
                out[i, pl.ds(at, 16)] = total.astype(BF)


def side_out(side_grad, partner, across):
    return call(side_body, [shaped(2, 64, LANES)] * 2, name="side_out")(side_grad, partner, across)


def final_body(own_grad, partner, across, from_prev, from_next, *refs):
    outs, total = refs[:GROUPS], refs[GROUPS]
    _, group, half, _ = place()
    spread = edge_pick(True)
    for i in range(2):
        edges = jnp.concatenate([from_prev[i], from_next[i]], axis=0)
        total[...] = own_grad[i] + jnp.dot(spread, edges, preferred_element_type=F32)
        for buf, low in ((partner, half), (across, 1 - half)):
            at = pl.ds(pl.multiple_of((1 - low) * 384, 128), 128)
            total[at, :] += buf[i, 0:128].astype(F32)
        for r, out in enumerate(outs):
            src = group ^ r
            for h in range(4):
                out[i, h] = total[pl.ds(spot(src, h), 32), :].astype(BF).reshape(2, 16, LANES)


def final(own_grad, partner, across, from_prev, from_next):
    return call(
        final_body, [shaped(*DEALT)] * GROUPS, [pltpu.VMEM((512, LANES), F32)], name="final"
    )(own_grad, partner, across, from_prev, from_next)


def local(queries, keys, values, out_grad, head_window):
    kv = deal(pack(keys, values, "pack_kv"), False)
    qd = deal(pack(queries, out_grad, "pack_qd"), False)
    own, first, last = own_kv(kv)
    left, right = cols_swap(first, last)
    partner, across = rows_swap(*rows_out(own, left, right))
    results = attend(head_window, own, left, right, partner, across, qd)
    oq = deal(results[:GROUPS], True)
    own_grad, side_grad, to_partner, to_across = results[GROUPS:]
    partner, across = rows_swap(to_partner, to_across)
    to_prev, to_next = side_out(side_grad, partner, across)
    from_prev, from_next = cols_swap(to_prev, to_next)
    dkv = deal(final(own_grad, partner, across, from_prev, from_next), True)
    attended, query_grad = unpack(oq, "unpack_oq")
    key_grad, value_grad = unpack(dkv, "unpack_dkv")
    return attended, query_grad, key_grad, value_grad


def solution(mesh):
    spec = P("ta", "ha", "wa", None)
    return jax.shard_map(
        local,
        mesh=mesh,
        in_specs=(spec,) * 4 + (P(),),
        out_specs=(spec,) * 4,
        check_vma=False,
    )
```

```python
from functools import partial
import math

import jax
import jax.numpy as jnp
from jax import lax
from jax.experimental import pallas as pl
from jax.experimental.pallas import tpu as pltpu
from jax.sharding import PartitionSpec as P

NEG = -1e30
BF = jnp.bfloat16
F32 = jnp.float32

GROUPS = 4
LANES = 384
HEAD = 128
GH = LANES // HEAD
ALL = ("ta", "ha", "wa")


DEAL = (
    (
        ((2, 1, 0, 3), (3, 2, 1, 0), (0, 3, 2, 1), (1, 0, 3, 2)),
        ((2, 1, 0, 3), (3, 0, 1, 2), (0, 3, 2, 1), (1, 2, 3, 0)),
    ),
    (
        ((0, 3, 2, 1), (1, 0, 3, 2), (2, 1, 0, 3), (3, 2, 1, 0)),
        ((0, 3, 2, 1), (3, 2, 1, 0), (2, 1, 0, 3), (1, 0, 3, 2)),
    ),
)


def code(turns):
    bits = sum(turns[r][i] << 2 * (4 * r + i) for r in range(4) for i in range(4))
    return bits - (1 << 32) if bits >= 1 << 31 else bits


def inverse(turns):
    return [[row.index(g) for g in range(4)] for row in turns]


def place():
    ta, ha, wa = (lax.axis_index(n) for n in ALL)
    z, y = ta * 4 + ha % 4, wa // 2
    return z // 2, wa % 2, (z + y) % 2, ha // 4


def looked_up(parity, half, table_of, at):
    which = parity * 2 + half
    bits = jnp.int32(code(table_of(DEAL[0][0])))
    for n in range(1, 4):
        bits = jnp.where(which == n, jnp.int32(code(table_of(DEAL[n // 2][n % 2]))), bits)
    return [lax.shift_right_logical(bits, 2 * (4 * r + at)) & 3 for r in range(GROUPS)]


def groups_out():
    ta, ha, wa = (lax.axis_index(n) for n in ALL)
    return looked_up((wa // 2 + wa) % 2, ha % 4 // 2, lambda t: t, ta * 2 + ha % 2)


def blocks_in():
    ta, ha, wa = (lax.axis_index(n) for n in ALL)
    return looked_up(ha % 2, wa % 2, inverse, (ta * 4 + ha % 4) // 2)


def lin(x, y, z, core):
    return (z // 4) * 128 + (x * 4 + z % 4) * 8 + y * 2 + core


EVERY = [(x, y, z, c) for x in range(4) for y in range(4) for z in range(8) for c in range(2)]


def deal_pairs(turn, back):
    pairs = []
    for x, y, z, core in EVERY:
        parity, half = (core + y) % 2, z % 4 // 2
        group = DEAL[parity][half][turn][(z // 4) * 2 + z % 2]
        pair = (lin(x, y, z, core), lin(x, y, 2 * group + parity, half))
        pairs.append(pair[::-1] if back else pair)
    return pairs


def deal(bufs, back):
    return [lax.ppermute(b, ALL, deal_pairs(r, back)) for r, b in enumerate(bufs)]


def swap(buf, partner_of):
    pairs = []
    for x, y, z, core in EVERY:
        x2, y2, z2, core2 = partner_of(x, y, z, core)
        if 0 <= x2 < 4 and 0 <= y2 < 4:
            pairs.append((lin(x, y, z, core), lin(x2, y2, z2, core2)))
    return lax.ppermute(buf, ALL, pairs)


def rows_swap(inner, outer):
    return (
        swap(inner, lambda x, y, z, c: (x, y, z, 1 - c)),
        swap(outer, lambda x, y, z, c: (x + 2 * c - 1, y, z, 1 - c)),
    )


def cols_swap(inner, outer):
    return (
        swap(inner, lambda x, y, z, c: (x, y, z ^ 1, c)),
        swap(outer, lambda x, y, z, c: (x, y + 2 * ((z + y) % 2) - 1, z, c)),
    )


def ordered(first, later):
    got = lax.optimization_barrier((first[0],) + tuple(later))
    return [got[0]] + list(first[1:]), list(got[1:])


def call(body, outs, scratch=(), flops=0, size=3 << 20, name=None, **specs):
    return pl.pallas_call(
        body,
        out_shape=outs,
        scratch_shapes=list(scratch),
        compiler_params=pltpu.CompilerParams(vmem_limit_bytes=48 << 20),
        cost_estimate=pl.CostEstimate(flops=flops, bytes_accessed=size, transcendentals=0),
        name=name,
        **specs,
    )


def shaped(*dims, dtype=BF):
    return jax.ShapeDtypeStruct(dims, dtype)


DEALT = (2, 2, 4, 16, LANES)
FAR = pl.BlockSpec(memory_space=pltpu.HBM)
NEAR = pl.BlockSpec(memory_space=pltpu.VMEM)


def lanes_of(group):
    return pl.ds(pl.multiple_of(group * LANES, LANES), LANES)


def run_copies(pairs, sems):
    copies = [pltpu.make_async_copy(a, b, sems.at[n]) for n, (a, b) in enumerate(pairs)]
    for c in copies:
        c.start()
    for c in copies:
        c.wait()


def pack_body(*refs):
    ins, outs, sems = refs[:2], refs[2:-1], refs[-1]
    run_copies(
        [
            (ref.at[:, :, :, lanes_of(group)], out.at[i])
            for group, out in zip(groups_out(), outs)
            for i, ref in enumerate(ins)
        ],
        sems,
    )


def pack(a, b, name):
    return call(
        pack_body,
        [shaped(*DEALT)] * GROUPS,
        [pltpu.SemaphoreType.DMA((2 * GROUPS,))],
        in_specs=[FAR] * 2,
        out_specs=[NEAR] * GROUPS,
        name=name,
    )(a, b)


def unpack_body(*refs):
    bufs, outs, sems = refs[:GROUPS], refs[GROUPS:-1], refs[-1]
    run_copies(
        [
            (buf.at[i], ref.at[:, :, :, lanes_of(group)])
            for group, buf in zip(groups_out(), bufs)
            for i, ref in enumerate(outs)
        ],
        sems,
    )


def unpack(bufs, name):
    return call(
        unpack_body,
        [shaped(2, 4, 16, GROUPS * LANES)] * 2,
        [pltpu.SemaphoreType.DMA((2 * GROUPS,))],
        in_specs=[NEAR] * GROUPS,
        out_specs=[FAR] * 2,
        name=name,
    )(*bufs)


def spot(src, t, h):
    return pl.ds(pl.multiple_of((src % 2) * 256 + (src // 2) * 32 + h * 64 + t * 16, 16), 16)


BLOCK = [(t, h) for t in range(2) for h in range(4)]


def gather_blocks(bufs, i, dest):
    for src, buf in zip(blocks_in(), bufs):
        for t, h in BLOCK:
            dest[i, spot(src, t, h), :] = buf[i, t, h]


def edge_pick(transpose):
    shape = (512, 128) if transpose else (128, 512)
    e = lax.broadcasted_iota(jnp.int32, shape, 1 if transpose else 0)
    token = lax.broadcasted_iota(jnp.int32, shape, 0 if transpose else 1)
    want = (e % 64) // 2 * 16 + e % 2 + 14 * (e // 64)
    return jnp.where(token == want, 1.0, 0.0).astype(BF)


def side_slots(block):
    return 1 - block, block


def row_slots(half):
    return 1 - half, half


def at_16(start, size=16):
    return pl.ds(pl.multiple_of(start, 16), size)


def own_body(*refs):
    bufs, (own, *outs), edges = refs[:GROUPS], refs[GROUPS:-1], refs[-1]
    _, _, block, _ = place()
    pick = edge_pick(False)
    for i in range(2):
        gather_blocks(bufs, i, own)
        both = jnp.dot(pick, own[i], preferred_element_type=F32).astype(BF)
        edges[0, i] = both[:64]
        edges[1, i] = both[64:]
    for out, slot in zip(outs, side_slots(block)):
        out[...] = edges[slot]


def own_kv(bufs):
    outs = [shaped(2, 512, LANES), shaped(2, 64, LANES), shaped(2, 64, LANES)]
    return call(own_body, outs, [pltpu.VMEM((2, 2, 64, LANES), BF)], name="own_kv")(*bufs)


def rows_body(own, inner, outer, *outs):
    _, half, block, _ = place()
    for out, below in zip(outs, row_slots(half)):
        out[:, 0:128] = own[:, at_16(below * 384, 128)]
        for side, slot in zip((inner, outer), side_slots(block)):
            out[:, at_16(128 + slot * 16)] = side[:, at_16(below * 48)]


def rows_out(own, inner, outer):
    return call(rows_body, [shaped(2, 160, LANES)] * 2, name="rows_out")(own, inner, outer)


NT = (((1,), (1,)), ((), ()))
TN = (((0,), (0,)), ((), ()))


def attend_body(window, own, col_in, col_out, row_in, row_out, *refs):
    qd = refs[:GROUPS]
    back = refs[GROUPS : 2 * GROUPS]
    own_grad, side_grad, *rows_back = refs[2 * GROUPS : 2 * GROUPS + 4]
    kv_mid, kv_side, g_mid, g_side, q_all, o_all = refs[2 * GROUPS + 4 :]
    group, half, block, x = place()
    w_at = lax.axis_index("wa") // 2 * 2 + block
    w_last = lax.axis_size("wa") - 1
    scale = 1.0 / math.sqrt(HEAD)
    log2e = 1.0 / math.log(2.0)

    rows = list(zip((row_in, row_out), row_slots(half)))
    for i in range(2):
        kv_mid[i, 128:640] = own[i]
        for side, slot in zip((col_in, col_out), side_slots(block)):
            kv_side[slot, i, 16:80] = side[i]
        for buf, below in rows:
            kv_mid[i, at_16(below * 640, 128)] = buf[i, 0:128]
            for slot in range(2):
                kv_side[slot, i, at_16(below * 80)] = buf[i, 128 + 16 * slot : 144 + 16 * slot]
        gather_blocks(qd, i, q_all)

    qi = lax.broadcasted_iota(jnp.int32, (128, 1), 0)
    q_t, q_w = qi // 32 % 2, qi % 16 // 2
    ki = lax.broadcasted_iota(jnp.int32, (1, 480), 1)
    mid = ki < 384
    ks = jnp.where(ki < 432, ki - 384, ki - 432)
    k_t = jnp.where(mid, ki // 32 % 2, ks // 4 % 2)
    k_w = jnp.where(mid, ki % 16 // 2, jnp.where(ki < 432, -1, 8))
    k_h = jnp.where(mid, ki // 128, ks // 16)
    beside = ((k_w >= 0) | (w_at > 0)) & ((k_w < 8) | (w_at < w_last))
    tile_row = (x * 2 + half) * 4 - 1
    tile_rows = 4 * 8

    for n in range(GH):
        f = slice(n * HEAD, (n + 1) * HEAD)
        head = group * GH + n
        rad_t, rad_h, rad_w = window[head, 0], window[head, 1], window[head, 2]
        near = (jnp.abs(q_t - k_t) <= rad_t) & (jnp.abs(q_w - k_w) <= rad_w)
        base = jnp.where(near, 0.0, NEG)
        inside = beside & (jnp.abs(k_h - 1) <= rad_h)
        all_w, all_ds = [], []
        side_g = [[[None] * 6, [None] * 6], [[None] * 6, [None] * 6]]
        for blk in range(4):
            row = tile_row + blk + k_h
            row_bias = jnp.where(inside & (row >= 0) & (row < tile_rows), 0.0, NEG)
            mid_at, side_at, q_at = pl.ds(128 * blk, 384), pl.ds(16 * blk, 48), pl.ds(128 * blk, 128)
            k, v = (
                jnp.concatenate(
                    [kv_mid[i, mid_at, f], kv_side[0, i, side_at, f], kv_side[1, i, side_at, f]], axis=0
                )
                for i in range(2)
            )
            q, do = q_all[0, q_at, f], q_all[1, q_at, f]
            s = lax.dot_general(q, k, NT, preferred_element_type=F32)
            s = s * (scale * log2e) + (base + row_bias)
            top = jnp.max(s, axis=1, keepdims=True)
            e = jnp.exp2(s - top)
            p = e * (1.0 / jnp.sum(e, axis=1, keepdims=True))
            wts = p.astype(BF)
            o = jnp.dot(wts, v, preferred_element_type=F32).astype(BF)
            delta = jnp.sum(do.astype(F32) * o.astype(F32), axis=1, keepdims=True)
            dp = lax.dot_general(do, v, NT, preferred_element_type=F32)
            ds = (p * (dp - delta)).astype(BF)
            dq = jnp.dot(ds, k, preferred_element_type=F32) * scale
            o_all[0, q_at, f] = o
            o_all[1, q_at, f] = dq.astype(BF)
            all_ds.append(ds)
            all_w.append(wts)
            for i, (a, b) in enumerate(((ds, q), (wts, do))):
                part = lax.dot_general(a[:, 384:480], b, TN, preferred_element_type=F32)
                for lr in range(2):
                    for o_ in range(3):
                        piece = part[48 * lr + 16 * o_ : 48 * lr + 16 * o_ + 16]
                        have = side_g[i][lr][blk + o_]
                        side_g[i][lr][blk + o_] = piece if have is None else have + piece
        for i, a in enumerate((all_ds, all_w)):
            mul = scale if i == 0 else 1.0
            for j in range(6):
                blks = [b for b in range(4) if 0 <= j - b <= 2]
                lhs = [a[b][:, 128 * (j - b) : 128 * (j - b) + 128] for b in blks]
                lhs = lhs[0] if len(lhs) == 1 else jnp.concatenate(lhs, axis=0)
                rhs = q_all[i, pl.ds(128 * blks[0], 128 * len(blks)), f]
                g_mid[i, 128 * j : 128 * j + 128, f] = (
                    lax.dot_general(lhs, rhs, TN, preferred_element_type=F32) * mul
                )
                for slot in range(2):
                    g_side[slot, i, 16 * j : 16 * j + 16, f] = side_g[i][slot][j] * mul

    for src, out in zip(blocks_in(), back):
        for i in range(2):
            for t, h in BLOCK:
                out[i, t, h] = o_all[i, spot(src, t, h), :]
    for i in range(2):
        own_grad[i] = g_mid[i, 128:640]
        for slot in range(2):
            side_grad[slot, i] = g_side[slot, i, 16:80]
        for out, (_, below) in zip(rows_back, rows):
            out[i, 0:128] = g_mid[i, at_16(below * 640, 128)].astype(BF)
            for slot in range(2):
                out[i, 128 + 16 * slot : 144 + 16 * slot] = g_side[slot, i, at_16(below * 80)].astype(BF)


def attend(window, own, cols, rows, qd):
    outs = [shaped(*DEALT)] * GROUPS + [
        shaped(2, 512, LANES, dtype=F32),
        shaped(2, 2, 64, LANES, dtype=F32),
        shaped(2, 160, LANES),
        shaped(2, 160, LANES),
    ]
    ins = [own, *cols, *rows, *qd]
    scratch = [
        pltpu.VMEM((2, 768, LANES), BF),
        pltpu.VMEM((2, 2, 96, LANES), BF),
        pltpu.VMEM((2, 768, LANES), F32),
        pltpu.VMEM((2, 2, 96, LANES), F32),
        pltpu.VMEM((2, 512, LANES), BF),
        pltpu.VMEM((2, 512, LANES), BF),
    ]
    return call(
        attend_body,
        outs,
        scratch,
        in_specs=[pl.BlockSpec(memory_space=pltpu.SMEM)] + [NEAR] * len(ins),
        out_specs=[NEAR] * len(outs),
        flops=1200000000,
        size=8 << 20,
        name="attend",
    )(window, *ins)


def side_body(side_grad, row_in, row_out, *outs):
    _, half, block, _ = place()
    for out, slot in zip(outs, side_slots(block)):
        for i in range(2):
            out[i] = side_grad[slot, i].astype(BF)
            for buf, below in zip((row_in, row_out), row_slots(half)):
                at = at_16(below * 48)
                come = buf[i, at_16(128 + slot * 16)].astype(F32)
                out[i, at] = (side_grad[slot, i, at] + come).astype(BF)


def side_out(side_grad, rows):
    return call(side_body, [shaped(2, 64, LANES)] * 2, name="side_out")(side_grad, *rows)


def final_body(own_grad, row_in, row_out, col_in, col_out, *refs):
    outs, (total, edges) = refs[:GROUPS], refs[GROUPS:]
    _, half, block, _ = place()
    spread = edge_pick(True)
    for i in range(2):
        for side, slot in zip((col_in, col_out), side_slots(block)):
            edges[slot, i] = side[i]
        both = jnp.concatenate([edges[0, i], edges[1, i]], axis=0)
        total[i] = own_grad[i] + jnp.dot(spread, both, preferred_element_type=F32)
        for buf, below in zip((row_in, row_out), row_slots(half)):
            total[i, at_16(below * 384, 128), :] += buf[i, 0:128].astype(F32)
        for src, out in zip(blocks_in(), outs):
            for t, h in BLOCK:
                out[i, t, h] = total[i, spot(src, t, h), :].astype(BF)


def final(own_grad, rows, cols):
    scratch = [pltpu.VMEM((2, 512, LANES), F32), pltpu.VMEM((2, 2, 64, LANES), BF)]
    return call(final_body, [shaped(*DEALT)] * GROUPS, scratch, name="final")(own_grad, *rows, *cols)


def local(queries, keys, values, out_grad, head_window):
    sent = list(pack(keys, values, "pack_kv"))
    sent, (queries, out_grad) = ordered(sent, (queries, out_grad))
    kv = deal(sent, False)
    qd = deal(pack(queries, out_grad, "pack_qd"), False)
    kv, qd[:1] = ordered(kv, qd[:1])
    own, *edges = own_kv(kv)
    cols = cols_swap(*edges)
    cols, qd[1:] = ordered(cols, qd[1:])
    rows = rows_swap(*rows_out(own, *cols))
    results = attend(head_window, own, cols, rows, qd)
    oq = deal(results[:GROUPS], True)
    own_grad, side_grad, *rows_back = results[GROUPS:]
    rows = rows_swap(*rows_back)
    cols = cols_swap(*side_out(side_grad, rows))
    dkv = deal(final(own_grad, rows, cols), True)
    attended, query_grad = unpack(oq, "unpack_oq")
    key_grad, value_grad = unpack(dkv, "unpack_dkv")
    return attended, query_grad, key_grad, value_grad


def solution(mesh):
    spec = P("ta", "ha", "wa", None)
    return jax.shard_map(
        local,
        mesh=mesh,
        in_specs=(spec,) * 4 + (P(),),
        out_specs=(spec,) * 4,
        check_vma=False,
    )
```

```python
from functools import partial
import math

import jax
import jax.numpy as jnp
from jax import lax
from jax.experimental import pallas as pl
from jax.experimental.pallas import tpu as pltpu
from jax.sharding import PartitionSpec as P

NEG = -1e30
BF = jnp.bfloat16
F32 = jnp.float32

GROUPS = 4
LANES = 384
HEAD = 128
GH = LANES // HEAD
ALL = ("ta", "ha", "wa")


DEAL = (
    (
        ((2, 1, 0, 3), (3, 2, 1, 0), (0, 3, 2, 1), (1, 0, 3, 2)),
        ((2, 1, 0, 3), (3, 0, 1, 2), (0, 3, 2, 1), (1, 2, 3, 0)),
    ),
    (
        ((0, 3, 2, 1), (1, 0, 3, 2), (2, 1, 0, 3), (3, 2, 1, 0)),
        ((0, 3, 2, 1), (3, 2, 1, 0), (2, 1, 0, 3), (1, 0, 3, 2)),
    ),
)


def code(turns):
    bits = sum(turns[r][i] << 2 * (4 * r + i) for r in range(4) for i in range(4))
    return bits - (1 << 32) if bits >= 1 << 31 else bits


def inverse(turns):
    return [[row.index(g) for g in range(4)] for row in turns]


def place():
    ta, ha, wa = (lax.axis_index(n) for n in ALL)
    z, y = ta * 4 + ha % 4, wa // 2
    return z // 2, wa % 2, (z + y) % 2, ha // 4


def looked_up(parity, half, table_of, at):
    which = parity * 2 + half
    bits = jnp.int32(code(table_of(DEAL[0][0])))
    for n in range(1, 4):
        bits = jnp.where(which == n, jnp.int32(code(table_of(DEAL[n // 2][n % 2]))), bits)
    return [lax.shift_right_logical(bits, 2 * (4 * r + at)) & 3 for r in range(GROUPS)]


def groups_out():
    ta, ha, wa = (lax.axis_index(n) for n in ALL)
    return looked_up((wa // 2 + wa) % 2, ha % 4 // 2, lambda t: t, ta * 2 + ha % 2)


def blocks_in():
    ta, ha, wa = (lax.axis_index(n) for n in ALL)
    return looked_up(ha % 2, wa % 2, inverse, (ta * 4 + ha % 4) // 2)


def lin(x, y, z, core):
    return (z // 4) * 128 + (x * 4 + z % 4) * 8 + y * 2 + core


EVERY = [(x, y, z, c) for x in range(4) for y in range(4) for z in range(8) for c in range(2)]


def deal_pairs(turn, back):
    pairs = []
    for x, y, z, core in EVERY:
        parity, half = (core + y) % 2, z % 4 // 2
        group = DEAL[parity][half][turn][(z // 4) * 2 + z % 2]
        pair = (lin(x, y, z, core), lin(x, y, 2 * group + parity, half))
        pairs.append(pair[::-1] if back else pair)
    return pairs


def deal(bufs, back):
    return [lax.ppermute(b, ALL, deal_pairs(r, back)) for r, b in enumerate(bufs)]


def swap(buf, partner_of):
    pairs = []
    for x, y, z, core in EVERY:
        x2, y2, z2, core2 = partner_of(x, y, z, core)
        if 0 <= x2 < 4 and 0 <= y2 < 4:
            pairs.append((lin(x, y, z, core), lin(x2, y2, z2, core2)))
    return lax.ppermute(buf, ALL, pairs)


def rows_swap(inner, outer):
    return (
        swap(inner, lambda x, y, z, c: (x, y, z, 1 - c)),
        swap(outer, lambda x, y, z, c: (x + 2 * c - 1, y, z, 1 - c)),
    )


def cols_swap(inner, outer):
    return (
        swap(inner, lambda x, y, z, c: (x, y, z ^ 1, c)),
        swap(outer, lambda x, y, z, c: (x, y + 2 * ((z + y) % 2) - 1, z, c)),
    )


def ordered(first, later):
    got = lax.optimization_barrier((first[0],) + tuple(later))
    return [got[0]] + list(first[1:]), list(got[1:])


def call(body, outs, scratch=(), flops=0, size=3 << 20, name=None, **specs):
    return pl.pallas_call(
        body,
        out_shape=outs,
        scratch_shapes=list(scratch),
        compiler_params=pltpu.CompilerParams(vmem_limit_bytes=48 << 20),
        cost_estimate=pl.CostEstimate(flops=flops, bytes_accessed=size, transcendentals=0),
        name=name,
        **specs,
    )


def shaped(*dims, dtype=BF):
    return jax.ShapeDtypeStruct(dims, dtype)


DEALT = (2, 2, 4, 16, LANES)
FAR = pl.BlockSpec(memory_space=pltpu.HBM)
NEAR = pl.BlockSpec(memory_space=pltpu.VMEM)


def lanes_of(group):
    return pl.ds(pl.multiple_of(group * LANES, LANES), LANES)


def run_copies(pairs, sems):
    copies = [pltpu.make_async_copy(a, b, sems.at[n]) for n, (a, b) in enumerate(pairs)]
    for c in copies:
        c.start()
    for c in copies:
        c.wait()


def pack_body(*refs):
    ins, outs, sems = refs[:2], refs[2:-1], refs[-1]
    run_copies(
        [
            (ref.at[:, :, :, lanes_of(group)], out.at[i])
            for group, out in zip(groups_out(), outs)
            for i, ref in enumerate(ins)
        ],
        sems,
    )


def pack(a, b, name):
    return call(
        pack_body,
        [shaped(*DEALT)] * GROUPS,
        [pltpu.SemaphoreType.DMA((2 * GROUPS,))],
        in_specs=[FAR] * 2,
        out_specs=[NEAR] * GROUPS,
        name=name,
    )(a, b)


def unpack_body(*refs):
    bufs, outs, sems = refs[:GROUPS], refs[GROUPS:-1], refs[-1]
    run_copies(
        [
            (buf.at[i], ref.at[:, :, :, lanes_of(group)])
            for group, buf in zip(groups_out(), bufs)
            for i, ref in enumerate(outs)
        ],
        sems,
    )


def unpack(bufs, name):
    return call(
        unpack_body,
        [shaped(2, 4, 16, GROUPS * LANES)] * 2,
        [pltpu.SemaphoreType.DMA((2 * GROUPS,))],
        in_specs=[NEAR] * GROUPS,
        out_specs=[FAR] * 2,
        name=name,
    )(*bufs)


def spot(src, t, h):
    return pl.ds(pl.multiple_of((src % 2) * 256 + (src // 2) * 32 + h * 64 + t * 16, 16), 16)


BLOCK = [(t, h) for t in range(2) for h in range(4)]


def gather_blocks(bufs, i, dest):
    for src, buf in zip(blocks_in(), bufs):
        for t, h in BLOCK:
            dest[i, spot(src, t, h), :] = buf[i, t, h]


def edge_pick(transpose):
    shape = (512, 128) if transpose else (128, 512)
    e = lax.broadcasted_iota(jnp.int32, shape, 1 if transpose else 0)
    token = lax.broadcasted_iota(jnp.int32, shape, 0 if transpose else 1)
    want = (e % 64) // 2 * 16 + e % 2 + 14 * (e // 64)
    return jnp.where(token == want, 1.0, 0.0).astype(BF)


def side_slots(block):
    return 1 - block, block


def row_slots(half):
    return 1 - half, half


def at_16(start, size=16):
    return pl.ds(pl.multiple_of(start, 16), size)


def own_body(*refs):
    bufs, (own, *outs), edges = refs[:GROUPS], refs[GROUPS:-1], refs[-1]
    _, _, block, _ = place()
    pick = edge_pick(False)
    for i in range(2):
        gather_blocks(bufs, i, own)
        both = jnp.dot(pick, own[i], preferred_element_type=F32).astype(BF)
        edges[0, i] = both[:64]
        edges[1, i] = both[64:]
    for out, slot in zip(outs, side_slots(block)):
        out[...] = edges[slot]


def own_kv(bufs):
    outs = [shaped(2, 512, LANES), shaped(2, 64, LANES), shaped(2, 64, LANES)]
    return call(own_body, outs, [pltpu.VMEM((2, 2, 64, LANES), BF)], name="own_kv")(*bufs)


def rows_body(own, inner, outer, *outs):
    _, half, block, _ = place()
    for out, below in zip(outs, row_slots(half)):
        out[:, 0:128] = own[:, at_16(below * 384, 128)]
        for side, slot in zip((inner, outer), side_slots(block)):
            out[:, at_16(128 + slot * 16)] = side[:, at_16(below * 48)]


def rows_out(own, inner, outer):
    return call(rows_body, [shaped(2, 160, LANES)] * 2, name="rows_out")(own, inner, outer)


NT = (((1,), (1,)), ((), ()))
TN = (((0,), (0,)), ((), ()))


def row_sums(x):
    high = x.astype(BF)
    low = (x - high.astype(F32)).astype(BF)
    ones = jnp.ones((16, HEAD), BF)
    sums = lax.dot_general(ones, high, NT, preferred_element_type=F32)
    sums += lax.dot_general(ones, low, NT, preferred_element_type=F32)
    return sums[0:1]


def attend_body(window, own, col_in, col_out, row_in, row_out, *refs):
    qd = refs[:GROUPS]
    back = refs[GROUPS : 2 * GROUPS]
    own_grad, side_grad, *rows_back = refs[2 * GROUPS : 2 * GROUPS + 4]
    kv_mid, kv_side, g_mid, g_side, q_all, o_all = refs[2 * GROUPS + 4 :]
    group, half, block, x = place()
    w_at = lax.axis_index("wa") // 2 * 2 + block
    w_last = lax.axis_size("wa") - 1
    scale = 1.0 / math.sqrt(HEAD)
    log2e = 1.0 / math.log(2.0)

    rows = list(zip((row_in, row_out), row_slots(half)))
    for i in range(2):
        kv_mid[i, 128:640] = own[i]
        for side, slot in zip((col_in, col_out), side_slots(block)):
            kv_side[slot, i, 16:80] = side[i]
        for buf, below in rows:
            kv_mid[i, at_16(below * 640, 128)] = buf[i, 0:128]
            for slot in range(2):
                kv_side[slot, i, at_16(below * 80)] = buf[i, 128 + 16 * slot : 144 + 16 * slot]
        gather_blocks(qd, i, q_all)

    qi = lax.broadcasted_iota(jnp.int32, (1, 128), 1)
    q_t, q_w = qi // 32 % 2, qi % 16 // 2
    ki = lax.broadcasted_iota(jnp.int32, (160, 1), 0)
    mid = ki < 128
    ks = jnp.where(ki < 144, ki - 128, ki - 144)
    k_t = jnp.where(mid, ki // 32 % 2, ks // 4 % 2)
    k_w = jnp.where(mid, ki % 16 // 2, jnp.where(ki < 144, -1, 8))
    beside = ((k_w >= 0) | (w_at > 0)) & ((k_w < 8) | (w_at < w_last))
    t_far, w_far = jnp.abs(q_t - k_t), jnp.where(beside, jnp.abs(q_w - k_w), 99)
    tile_row = (x * 2 + half) * 4 - 1
    tile_rows = 4 * 8

    for n in range(GH):
        f = slice(n * HEAD, (n + 1) * HEAD)
        head = group * GH + n
        rad_t, rad_h, rad_w = window[head, 0], window[head, 1], window[head, 2]
        base = jnp.where((t_far <= rad_t) & (w_far <= rad_w), 0.0, NEG)
        all_w, all_ds, held = [], [], []
        side_g = [[[None] * 6, [None] * 6], [[None] * 6, [None] * 6]]
        for blk in range(4):
            biases = []
            for j in range(3):
                row = tile_row + blk + j
                seen = (row >= 0) & (row < tile_rows) & (abs(j - 1) <= rad_h)
                biases.append(base + jnp.where(seen, 0.0, NEG))
            bias = jnp.concatenate(
                [biases[j][lo:hi] for lo, hi in ((0, 128), (128, 144), (144, 160)) for j in range(3)],
                axis=0,
            )
            mid_at, side_at, q_at = pl.ds(128 * blk, 384), pl.ds(16 * blk, 48), pl.ds(128 * blk, 128)
            k, v = (
                jnp.concatenate(
                    [kv_mid[i, mid_at, f], kv_side[0, i, side_at, f], kv_side[1, i, side_at, f]], axis=0
                )
                for i in range(2)
            )
            q, do = q_all[0, q_at, f], q_all[1, q_at, f]
            s = lax.dot_general(k, q, NT, preferred_element_type=F32)
            dp = lax.dot_general(v, do, NT, preferred_element_type=F32)
            held.append((k, v, q, do, s, dp, bias))
        soft = []
        for blk, (k, v, q, do, s, dp, bias) in enumerate(held):
            s = s * (scale * log2e) + bias
            e = jnp.exp2(s - jnp.max(s, axis=0, keepdims=True))
            p = e * (1.0 / jnp.sum(e, axis=0, keepdims=True))
            wts = p.astype(BF)
            o = lax.dot_general(wts, v, TN, preferred_element_type=F32).astype(BF)
            o_all[0, pl.ds(128 * blk, 128), f] = o
            soft.append((p, wts, row_sums(do.astype(F32) * o.astype(F32))))
        for blk, (k, v, q, do, s, dp, bias) in enumerate(held):
            p, wts, delta = soft[blk]
            ds = (p * (dp - delta)).astype(BF)
            dq = lax.dot_general(ds, k, TN, preferred_element_type=F32) * scale
            o_all[1, pl.ds(128 * blk, 128), f] = dq.astype(BF)
            all_ds.append(ds)
            all_w.append(wts)
            for i, (a, b) in enumerate(((ds, q), (wts, do))):
                part = jnp.dot(a[384:480], b, preferred_element_type=F32)
                for lr in range(2):
                    for o_ in range(3):
                        piece = part[48 * lr + 16 * o_ : 48 * lr + 16 * o_ + 16]
                        have = side_g[i][lr][blk + o_]
                        side_g[i][lr][blk + o_] = piece if have is None else have + piece
        for i, a in enumerate((all_ds, all_w)):
            mul = scale if i == 0 else 1.0
            for j in range(6):
                blks = [b for b in range(4) if 0 <= j - b <= 2]
                lhs = [a[b][128 * (j - b) : 128 * (j - b) + 128] for b in blks]
                lhs = lhs[0] if len(lhs) == 1 else jnp.concatenate(lhs, axis=1)
                rhs = q_all[i, pl.ds(128 * blks[0], 128 * len(blks)), f]
                g_mid[i, 128 * j : 128 * j + 128, f] = (
                    jnp.dot(lhs, rhs, preferred_element_type=F32) * mul
                )
                for slot in range(2):
                    g_side[slot, i, 16 * j : 16 * j + 16, f] = side_g[i][slot][j] * mul

    for src, out in zip(blocks_in(), back):
        for i in range(2):
            for t, h in BLOCK:
                out[i, t, h] = o_all[i, spot(src, t, h), :]
    for i in range(2):
        own_grad[i] = g_mid[i, 128:640]
        for slot in range(2):
            side_grad[slot, i] = g_side[slot, i, 16:80]
        for out, (_, below) in zip(rows_back, rows):
            out[i, 0:128] = g_mid[i, at_16(below * 640, 128)].astype(BF)
            for slot in range(2):
                out[i, 128 + 16 * slot : 144 + 16 * slot] = g_side[slot, i, at_16(below * 80)].astype(BF)


def attend(window, own, cols, rows, qd):
    outs = [shaped(*DEALT)] * GROUPS + [
        shaped(2, 512, LANES, dtype=F32),
        shaped(2, 2, 64, LANES, dtype=F32),
        shaped(2, 160, LANES),
        shaped(2, 160, LANES),
    ]
    ins = [own, *cols, *rows, *qd]
    scratch = [
        pltpu.VMEM((2, 768, LANES), BF),
        pltpu.VMEM((2, 2, 96, LANES), BF),
        pltpu.VMEM((2, 768, LANES), F32),
        pltpu.VMEM((2, 2, 96, LANES), F32),
        pltpu.VMEM((2, 512, LANES), BF),
        pltpu.VMEM((2, 512, LANES), BF),
    ]
    return call(
        attend_body,
        outs,
        scratch,
        in_specs=[pl.BlockSpec(memory_space=pltpu.SMEM)] + [NEAR] * len(ins),
        out_specs=[NEAR] * len(outs),
        flops=1200000000,
        size=8 << 20,
        name="attend",
    )(window, *ins)


def side_body(side_grad, row_in, row_out, *outs):
    _, half, block, _ = place()
    for out, slot in zip(outs, side_slots(block)):
        for i in range(2):
            out[i] = side_grad[slot, i].astype(BF)
            for buf, below in zip((row_in, row_out), row_slots(half)):
                at = at_16(below * 48)
                come = buf[i, at_16(128 + slot * 16)].astype(F32)
                out[i, at] = (side_grad[slot, i, at] + come).astype(BF)


def side_out(side_grad, rows):
    return call(side_body, [shaped(2, 64, LANES)] * 2, name="side_out")(side_grad, *rows)


def final_body(own_grad, row_in, row_out, col_in, col_out, *refs):
    outs, (total, edges) = refs[:GROUPS], refs[GROUPS:]
    _, half, block, _ = place()
    spread = edge_pick(True)
    for i in range(2):
        for side, slot in zip((col_in, col_out), side_slots(block)):
            edges[slot, i] = side[i]
        both = jnp.concatenate([edges[0, i], edges[1, i]], axis=0)
        total[i] = own_grad[i] + jnp.dot(spread, both, preferred_element_type=F32)
        for buf, below in zip((row_in, row_out), row_slots(half)):
            total[i, at_16(below * 384, 128), :] += buf[i, 0:128].astype(F32)
        for src, out in zip(blocks_in(), outs):
            for t, h in BLOCK:
                out[i, t, h] = total[i, spot(src, t, h), :].astype(BF)


def final(own_grad, rows, cols):
    scratch = [pltpu.VMEM((2, 512, LANES), F32), pltpu.VMEM((2, 2, 64, LANES), BF)]
    return call(final_body, [shaped(*DEALT)] * GROUPS, scratch, name="final")(own_grad, *rows, *cols)


def local(queries, keys, values, out_grad, head_window):
    queries, keys, values, out_grad = (
        pltpu.with_memory_space_constraint(v, pltpu.HBM) for v in (queries, keys, values, out_grad)
    )
    sent = list(pack(keys, values, "pack_kv"))
    sent, (queries, out_grad) = ordered(sent, (queries, out_grad))
    kv = deal(sent, False)
    ask = list(pack(queries, out_grad, "pack_qd"))
    qd = deal(ask, False)
    kv, qd[:1] = ordered(kv, qd[:1])
    own, *edges = own_kv(kv)
    cols = cols_swap(*edges)
    cols, qd[1:] = ordered(cols, qd[1:])
    rows = rows_swap(*rows_out(own, *cols))
    results = attend(head_window, own, cols, rows, qd)
    oq = deal(results[:GROUPS], True)
    own_grad, side_grad, *rows_back = results[GROUPS:]
    rows = rows_swap(*rows_back)
    cols = cols_swap(*side_out(side_grad, rows))
    dkv = deal(final(own_grad, rows, cols), True)
    attended, query_grad = unpack(oq, "unpack_oq")
    key_grad, value_grad = unpack(dkv, "unpack_dkv")
    return attended, query_grad, key_grad, value_grad


def solution(mesh):
    spec = P("ta", "ha", "wa", None)
    return jax.shard_map(
        local,
        mesh=mesh,
        in_specs=(spec,) * 4 + (P(),),
        out_specs=(spec,) * 4,
        check_vma=False,
    )
```

```python
from functools import partial
import math

import jax
import jax.numpy as jnp
from jax import lax
from jax.experimental import pallas as pl
from jax.experimental.pallas import tpu as pltpu
from jax.sharding import PartitionSpec as P

NEG = -1e30
BF = jnp.bfloat16
F32 = jnp.float32

GROUPS = 4
LANES = 384
HEAD = 128
GH = LANES // HEAD
ALL = ("ta", "ha", "wa")


DEAL = (
    (
        ((2, 1, 0, 3), (3, 2, 1, 0), (0, 3, 2, 1), (1, 0, 3, 2)),
        ((2, 1, 0, 3), (3, 0, 1, 2), (0, 3, 2, 1), (1, 2, 3, 0)),
    ),
    (
        ((0, 3, 2, 1), (1, 0, 3, 2), (2, 1, 0, 3), (3, 2, 1, 0)),
        ((0, 3, 2, 1), (3, 2, 1, 0), (2, 1, 0, 3), (1, 0, 3, 2)),
    ),
)


def code(turns):
    bits = sum(turns[r][i] << 2 * (4 * r + i) for r in range(4) for i in range(4))
    return bits - (1 << 32) if bits >= 1 << 31 else bits


def inverse(turns):
    return [[row.index(g) for g in range(4)] for row in turns]


def place():
    ta, ha, wa = (lax.axis_index(n) for n in ALL)
    z, y = ta * 4 + ha % 4, wa // 2
    return z // 2, wa % 2, (z + y) % 2, ha // 4


def looked_up(parity, half, table_of, at):
    which = parity * 2 + half
    bits = jnp.int32(code(table_of(DEAL[0][0])))
    for n in range(1, 4):
        bits = jnp.where(which == n, jnp.int32(code(table_of(DEAL[n // 2][n % 2]))), bits)
    return [lax.shift_right_logical(bits, 2 * (4 * r + at)) & 3 for r in range(GROUPS)]


def groups_out():
    ta, ha, wa = (lax.axis_index(n) for n in ALL)
    return looked_up((wa // 2 + wa) % 2, ha % 4 // 2, lambda t: t, ta * 2 + ha % 2)


def blocks_in():
    ta, ha, wa = (lax.axis_index(n) for n in ALL)
    return looked_up(ha % 2, wa % 2, inverse, (ta * 4 + ha % 4) // 2)


def lin(x, y, z, core):
    return (z // 4) * 128 + (x * 4 + z % 4) * 8 + y * 2 + core


EVERY = [(x, y, z, c) for x in range(4) for y in range(4) for z in range(8) for c in range(2)]


def deal_pairs(turn, back):
    pairs = []
    for x, y, z, core in EVERY:
        parity, half = (core + y) % 2, z % 4 // 2
        group = DEAL[parity][half][turn][(z // 4) * 2 + z % 2]
        pair = (lin(x, y, z, core), lin(x, y, 2 * group + parity, half))
        pairs.append(pair[::-1] if back else pair)
    return pairs


def deal(bufs, back):
    return [lax.ppermute(b, ALL, deal_pairs(r, back)) for r, b in enumerate(bufs)]


def swap(buf, partner_of):
    pairs = []
    for x, y, z, core in EVERY:
        x2, y2, z2, core2 = partner_of(x, y, z, core)
        if 0 <= x2 < 4 and 0 <= y2 < 4:
            pairs.append((lin(x, y, z, core), lin(x2, y2, z2, core2)))
    return lax.ppermute(buf, ALL, pairs)


def rows_swap(inner, outer):
    return (
        swap(inner, lambda x, y, z, c: (x, y, z, 1 - c)),
        swap(outer, lambda x, y, z, c: (x + 2 * c - 1, y, z, 1 - c)),
    )


def cols_swap(inner, outer):
    return (
        swap(inner, lambda x, y, z, c: (x, y, z ^ 1, c)),
        swap(outer, lambda x, y, z, c: (x, y + 2 * ((z + y) % 2) - 1, z, c)),
    )


def ordered(first, later):
    got = lax.optimization_barrier((first[0],) + tuple(later))
    return [got[0]] + list(first[1:]), list(got[1:])


def call(body, outs, scratch=(), flops=0, size=3 << 20, name=None, **specs):
    return pl.pallas_call(
        body,
        out_shape=outs,
        scratch_shapes=list(scratch),
        compiler_params=pltpu.CompilerParams(vmem_limit_bytes=48 << 20),
        cost_estimate=pl.CostEstimate(flops=flops, bytes_accessed=size, transcendentals=0),
        name=name,
        **specs,
    )


def shaped(*dims, dtype=BF):
    return jax.ShapeDtypeStruct(dims, dtype)


DEALT = (2, 2, 4, 16, LANES)
FAR = pl.BlockSpec(memory_space=pltpu.HBM)
NEAR = pl.BlockSpec(memory_space=pltpu.VMEM)


def lanes_of(group):
    return pl.ds(pl.multiple_of(group * LANES, LANES), LANES)


def run_copies(pairs, sems):
    copies = [pltpu.make_async_copy(a, b, sems.at[n]) for n, (a, b) in enumerate(pairs)]
    for c in copies:
        c.start()
    for c in copies:
        c.wait()


def pack_body(*refs):
    ins, outs, sems = refs[:2], refs[2:-1], refs[-1]
    run_copies(
        [
            (ref.at[:, :, :, lanes_of(group)], out.at[i])
            for group, out in zip(groups_out(), outs)
            for i, ref in enumerate(ins)
        ],
        sems,
    )


def pack(a, b, name):
    return call(
        pack_body,
        [shaped(*DEALT)] * GROUPS,
        [pltpu.SemaphoreType.DMA((2 * GROUPS,))],
        in_specs=[FAR] * 2,
        out_specs=[NEAR] * GROUPS,
        name=name,
    )(a, b)


def unpack_body(*refs):
    bufs, outs, sems = refs[:GROUPS], refs[GROUPS:-1], refs[-1]
    run_copies(
        [
            (buf.at[i], ref.at[:, :, :, lanes_of(group)])
            for group, buf in zip(groups_out(), bufs)
            for i, ref in enumerate(outs)
        ],
        sems,
    )


def unpack(bufs, name):
    return call(
        unpack_body,
        [shaped(2, 4, 16, GROUPS * LANES)] * 2,
        [pltpu.SemaphoreType.DMA((2 * GROUPS,))],
        in_specs=[NEAR] * GROUPS,
        out_specs=[FAR] * 2,
        name=name,
    )(*bufs)


def spot(src, t, h):
    return pl.ds(pl.multiple_of((src % 2) * 256 + (src // 2) * 32 + h * 64 + t * 16, 16), 16)


BLOCK = [(t, h) for t in range(2) for h in range(4)]


def gather_blocks(bufs, i, dest):
    for src, buf in zip(blocks_in(), bufs):
        for t, h in BLOCK:
            dest[i, spot(src, t, h), :] = buf[i, t, h]


def edge_pick(transpose, rows=8):
    few, many = 16 * rows, 64 * rows
    shape = (many, few) if transpose else (few, many)
    e = lax.broadcasted_iota(jnp.int32, shape, 1 if transpose else 0)
    token = lax.broadcasted_iota(jnp.int32, shape, 0 if transpose else 1)
    want = e % (8 * rows) // 2 * 16 + e % 2 + 14 * (e // (8 * rows))
    return jnp.where(token == want, 1.0, 0.0).astype(BF)


def side_slots(block):
    return 1 - block, block


def row_slots(half):
    return 1 - half, half


def at_16(start, size=16):
    return pl.ds(pl.multiple_of(start, 16), size)


def own_body(*refs):
    bufs, (own, *outs), edges = refs[:GROUPS], refs[GROUPS:-1], refs[-1]
    _, _, block, _ = place()
    pick = edge_pick(False)
    for i in range(2):
        gather_blocks(bufs, i, own)
        both = jnp.dot(pick, own[i], preferred_element_type=F32).astype(BF)
        edges[0, i] = both[:64]
        edges[1, i] = both[64:]
    for out, slot in zip(outs, side_slots(block)):
        out[...] = edges[slot]


def own_kv(bufs):
    outs = [shaped(2, 512, LANES), shaped(2, 64, LANES), shaped(2, 64, LANES)]
    return call(own_body, outs, [pltpu.VMEM((2, 2, 64, LANES), BF)], name="own_kv")(*bufs)


def rows_body(own, inner, outer, *outs):
    _, half, block, _ = place()
    for out, below in zip(outs, row_slots(half)):
        out[:, 0:128] = own[:, at_16(below * 384, 128)]
        for side, slot in zip((inner, outer), side_slots(block)):
            out[:, at_16(128 + slot * 16)] = side[:, at_16(below * 48)]


def rows_out(own, inner, outer):
    return call(rows_body, [shaped(2, 160, LANES)] * 2, name="rows_out")(own, inner, outer)


NT = (((1,), (1,)), ((), ()))
TN = (((0,), (0,)), ((), ()))


def row_sums(x):
    high = x.astype(BF)
    low = (x - high.astype(F32)).astype(BF)
    ones = jnp.ones((16, HEAD), BF)
    sums = lax.dot_general(ones, high, NT, preferred_element_type=F32)
    sums += lax.dot_general(ones, low, NT, preferred_element_type=F32)
    return sums[0:1]


def attend_body(window, own, col_in, col_out, row_in, row_out, *refs):
    qd = refs[:GROUPS]
    back = refs[GROUPS : 2 * GROUPS]
    own_grad, rows_grad, *cols_back = refs[2 * GROUPS : 2 * GROUPS + 4]
    kv_mid, kv_side, g_mid, g_side, q_all, o_all = refs[2 * GROUPS + 4 :]
    group, half, block, x = place()
    w_at = lax.axis_index("wa") // 2 * 2 + block
    w_last = lax.axis_size("wa") - 1
    scale = 1.0 / math.sqrt(HEAD)
    log2e = 1.0 / math.log(2.0)

    rows = list(zip((row_in, row_out), row_slots(half)))
    for i in range(2):
        kv_mid[i, 128:640] = own[i]
        for side, slot in zip((col_in, col_out), side_slots(block)):
            kv_side[slot, i, 16:80] = side[i]
        for buf, below in rows:
            kv_mid[i, at_16(below * 640, 128)] = buf[i, 0:128]
            for slot in range(2):
                kv_side[slot, i, at_16(below * 80)] = buf[i, 128 + 16 * slot : 144 + 16 * slot]
        gather_blocks(qd, i, q_all)

    qi = lax.broadcasted_iota(jnp.int32, (1, 128), 1)
    q_t, q_w = qi // 32 % 2, qi % 16 // 2
    ki = lax.broadcasted_iota(jnp.int32, (160, 1), 0)
    mid = ki < 128
    ks = jnp.where(ki < 144, ki - 128, ki - 144)
    k_t = jnp.where(mid, ki // 32 % 2, ks // 4 % 2)
    k_w = jnp.where(mid, ki % 16 // 2, jnp.where(ki < 144, -1, 8))
    beside = ((k_w >= 0) | (w_at > 0)) & ((k_w < 8) | (w_at < w_last))
    t_far, w_far = jnp.abs(q_t - k_t), jnp.where(beside, jnp.abs(q_w - k_w), 99)
    tile_row = (x * 2 + half) * 4 - 1
    tile_rows = 4 * 8

    for n in range(GH):
        f = slice(n * HEAD, (n + 1) * HEAD)
        head = group * GH + n
        rad_t, rad_h, rad_w = window[head, 0], window[head, 1], window[head, 2]
        base = jnp.where((t_far <= rad_t) & (w_far <= rad_w), 0.0, NEG)
        all_w, all_ds, held = [], [], []
        side_g = [[[None] * 6, [None] * 6], [[None] * 6, [None] * 6]]
        for blk in range(4):
            biases = []
            for j in range(3):
                row = tile_row + blk + j
                seen = (row >= 0) & (row < tile_rows) & (abs(j - 1) <= rad_h)
                biases.append(base + jnp.where(seen, 0.0, NEG))
            bias = jnp.concatenate(
                [biases[j][lo:hi] for lo, hi in ((0, 128), (128, 144), (144, 160)) for j in range(3)],
                axis=0,
            )
            mid_at, side_at, q_at = pl.ds(128 * blk, 384), pl.ds(16 * blk, 48), pl.ds(128 * blk, 128)
            k, v = (
                jnp.concatenate(
                    [kv_mid[i, mid_at, f], kv_side[0, i, side_at, f], kv_side[1, i, side_at, f]], axis=0
                )
                for i in range(2)
            )
            q, do = q_all[0, q_at, f], q_all[1, q_at, f]
            s = lax.dot_general(k, q, NT, preferred_element_type=F32)
            dp = lax.dot_general(v, do, NT, preferred_element_type=F32)
            held.append((k, v, q, do, s, dp, bias))
        soft = []
        for blk, (k, v, q, do, s, dp, bias) in enumerate(held):
            s = s * (scale * log2e) + bias
            e = jnp.exp2(s - jnp.max(s, axis=0, keepdims=True))
            p = e * (1.0 / jnp.sum(e, axis=0, keepdims=True))
            wts = p.astype(BF)
            o = lax.dot_general(wts, v, TN, preferred_element_type=F32).astype(BF)
            o_all[0, pl.ds(128 * blk, 128), f] = o
            soft.append((p, wts, row_sums(do.astype(F32) * o.astype(F32))))
        for blk, (k, v, q, do, s, dp, bias) in enumerate(held):
            p, wts, delta = soft[blk]
            ds = (p * (dp - delta)).astype(BF)
            dq = lax.dot_general(ds, k, TN, preferred_element_type=F32) * scale
            o_all[1, pl.ds(128 * blk, 128), f] = dq.astype(BF)
            all_ds.append(ds)
            all_w.append(wts)
            for i, (a, b) in enumerate(((ds, q), (wts, do))):
                part = jnp.dot(a[384:480], b, preferred_element_type=F32)
                for lr in range(2):
                    for o_ in range(3):
                        piece = part[48 * lr + 16 * o_ : 48 * lr + 16 * o_ + 16]
                        have = side_g[i][lr][blk + o_]
                        side_g[i][lr][blk + o_] = piece if have is None else have + piece
        for i, a in enumerate((all_ds, all_w)):
            mul = scale if i == 0 else 1.0
            for j in range(6):
                blks = [b for b in range(4) if 0 <= j - b <= 2]
                lhs = [a[b][128 * (j - b) : 128 * (j - b) + 128] for b in blks]
                lhs = lhs[0] if len(lhs) == 1 else jnp.concatenate(lhs, axis=1)
                rhs = q_all[i, pl.ds(128 * blks[0], 128 * len(blks)), f]
                g_mid[i, 128 * j : 128 * j + 128, f] = (
                    jnp.dot(lhs, rhs, preferred_element_type=F32) * mul
                )
                for slot in range(2):
                    g_side[slot, i, 16 * j : 16 * j + 16, f] = side_g[i][slot][j] * mul

    for src, out in zip(blocks_in(), back):
        for i in range(2):
            for t, h in BLOCK:
                out[i, t, h] = o_all[i, spot(src, t, h), :]
    for i in range(2):
        own_grad[i] = g_mid[i, 128:640]
        for n, (_, below) in enumerate(rows):
            rows_grad[n, i] = g_mid[i, at_16(below * 640, 128)]
        for out, slot in zip(cols_back, side_slots(block)):
            out[i] = g_side[slot, i].astype(BF)


def attend(window, own, cols, rows, qd):
    outs = [shaped(*DEALT)] * GROUPS + [
        shaped(2, 512, LANES, dtype=F32),
        shaped(2, 2, 128, LANES, dtype=F32),
        shaped(2, 96, LANES),
        shaped(2, 96, LANES),
    ]
    ins = [own, *cols, *rows, *qd]
    scratch = [
        pltpu.VMEM((2, 768, LANES), BF),
        pltpu.VMEM((2, 2, 96, LANES), BF),
        pltpu.VMEM((2, 768, LANES), F32),
        pltpu.VMEM((2, 2, 96, LANES), F32),
        pltpu.VMEM((2, 512, LANES), BF),
        pltpu.VMEM((2, 512, LANES), BF),
    ]
    return call(
        attend_body,
        outs,
        scratch,
        in_specs=[pl.BlockSpec(memory_space=pltpu.SMEM)] + [NEAR] * len(ins),
        out_specs=[NEAR] * len(outs),
        flops=1200000000,
        size=8 << 20,
        name="attend",
    )(window, *ins)


def rows_back_body(rows_grad, col_in, col_out, *refs):
    outs, edges = refs[:2], refs[2]
    _, half, block, _ = place()
    spread = edge_pick(True, 2)
    for side, slot in zip((col_in, col_out), side_slots(block)):
        edges[slot] = side[...]
    for n, (out, below) in enumerate(zip(outs, row_slots(half))):
        for i in range(2):
            both = jnp.concatenate([edges[slot, i, at_16(below * 80)] for slot in range(2)], axis=0)
            total = rows_grad[n, i] + jnp.dot(spread, both, preferred_element_type=F32)
            out[i] = total.astype(BF)


def rows_back(rows_grad, cols):
    scratch = [pltpu.VMEM((2, 2, 96, LANES), BF)]
    return call(rows_back_body, [shaped(2, 128, LANES)] * 2, scratch, name="rows_back")(rows_grad, *cols)


def final_body(own_grad, row_in, row_out, col_in, col_out, *refs):
    outs, (total, edges) = refs[:GROUPS], refs[GROUPS:]
    _, half, block, _ = place()
    spread = edge_pick(True)
    for side, slot in zip((col_in, col_out), side_slots(block)):
        edges[slot] = side[:, 16:80]
    for i in range(2):
        both = jnp.concatenate([edges[0, i], edges[1, i]], axis=0)
        total[i] = own_grad[i] + jnp.dot(spread, both, preferred_element_type=F32)
        for buf, below in zip((row_in, row_out), row_slots(half)):
            total[i, at_16(below * 384, 128), :] += buf[i].astype(F32)
        for src, out in zip(blocks_in(), outs):
            for t, h in BLOCK:
                out[i, t, h] = total[i, spot(src, t, h), :].astype(BF)


def final(own_grad, rows, cols):
    scratch = [pltpu.VMEM((2, 512, LANES), F32), pltpu.VMEM((2, 2, 64, LANES), BF)]
    return call(final_body, [shaped(*DEALT)] * GROUPS, scratch, name="final")(own_grad, *rows, *cols)


def local(queries, keys, values, out_grad, head_window):
    queries, keys, values, out_grad = (
        pltpu.with_memory_space_constraint(v, pltpu.HBM) for v in (queries, keys, values, out_grad)
    )
    sent = list(pack(keys, values, "pack_kv"))
    sent, (queries, out_grad) = ordered(sent, (queries, out_grad))
    kv = deal(sent, False)
    ask = list(pack(queries, out_grad, "pack_qd"))
    qd = deal(ask, False)
    kv, qd[:1] = ordered(kv, qd[:1])
    own, *edges = own_kv(kv)
    cols = cols_swap(*edges)
    cols, qd[1:] = ordered(cols, qd[1:])
    rows = rows_swap(*rows_out(own, *cols))
    results = attend(head_window, own, cols, rows, qd)
    oq = deal(results[:GROUPS], True)
    own_grad, rows_grad, *cols_back = results[GROUPS:]
    cols = cols_swap(*cols_back)
    rows = rows_swap(*rows_back(rows_grad, cols))
    rows, oq[0:2] = ordered(rows, oq[0:2])
    dkv = deal(final(own_grad, rows, cols), True)
    attended, query_grad = unpack(oq, "unpack_oq")
    key_grad, value_grad = unpack(dkv, "unpack_dkv")
    return attended, query_grad, key_grad, value_grad


def solution(mesh):
    spec = P("ta", "ha", "wa", None)
    return jax.shard_map(
        local,
        mesh=mesh,
        in_specs=(spec,) * 4 + (P(),),
        out_specs=(spec,) * 4,
        check_vma=False,
    )
```

```python
from functools import partial
import math

import jax
import jax.numpy as jnp
from jax import lax
from jax.experimental import pallas as pl
from jax.experimental.pallas import tpu as pltpu
from jax.sharding import PartitionSpec as P

NEG = -1e30
BF = jnp.bfloat16
F32 = jnp.float32

GROUPS = 4
LANES = 384
HEAD = 128
GH = LANES // HEAD
ALL = ("ta", "ha", "wa")


DEAL = (
    (
        ((2, 1, 0, 3), (3, 2, 1, 0), (0, 3, 2, 1), (1, 0, 3, 2)),
        ((2, 1, 0, 3), (3, 0, 1, 2), (0, 3, 2, 1), (1, 2, 3, 0)),
    ),
    (
        ((0, 3, 2, 1), (1, 0, 3, 2), (2, 1, 0, 3), (3, 2, 1, 0)),
        ((0, 3, 2, 1), (3, 2, 1, 0), (2, 1, 0, 3), (1, 0, 3, 2)),
    ),
)


def code(turns):
    bits = sum(turns[r][i] << 2 * (4 * r + i) for r in range(4) for i in range(4))
    return bits - (1 << 32) if bits >= 1 << 31 else bits


def inverse(turns):
    return [[row.index(g) for g in range(4)] for row in turns]


def place():
    ta, ha, wa = (lax.axis_index(n) for n in ALL)
    z, y = ta * 4 + ha % 4, wa // 2
    return z // 2, wa % 2, (z + y) % 2, ha // 4


def looked_up(parity, half, table_of, at):
    which = parity * 2 + half
    bits = jnp.int32(code(table_of(DEAL[0][0])))
    for n in range(1, 4):
        bits = jnp.where(which == n, jnp.int32(code(table_of(DEAL[n // 2][n % 2]))), bits)
    return [lax.shift_right_logical(bits, 2 * (4 * r + at)) & 3 for r in range(GROUPS)]


def groups_out():
    ta, ha, wa = (lax.axis_index(n) for n in ALL)
    return looked_up((wa // 2 + wa) % 2, ha % 4 // 2, lambda t: t, ta * 2 + ha % 2)


def blocks_in():
    ta, ha, wa = (lax.axis_index(n) for n in ALL)
    return looked_up(ha % 2, wa % 2, inverse, (ta * 4 + ha % 4) // 2)


def lin(x, y, z, core):
    return (z // 4) * 128 + (x * 4 + z % 4) * 8 + y * 2 + core


EVERY = [(x, y, z, c) for x in range(4) for y in range(4) for z in range(8) for c in range(2)]


def deal_pairs(turn, back):
    pairs = []
    for x, y, z, core in EVERY:
        parity, half = (core + y) % 2, z % 4 // 2
        group = DEAL[parity][half][turn][(z // 4) * 2 + z % 2]
        pair = (lin(x, y, z, core), lin(x, y, 2 * group + parity, half))
        pairs.append(pair[::-1] if back else pair)
    return pairs


def deal(bufs, back):
    return [lax.ppermute(b, ALL, deal_pairs(r, back)) for r, b in enumerate(bufs)]


def swap(buf, partner_of):
    pairs = []
    for x, y, z, core in EVERY:
        x2, y2, z2, core2 = partner_of(x, y, z, core)
        if 0 <= x2 < 4 and 0 <= y2 < 4:
            pairs.append((lin(x, y, z, core), lin(x2, y2, z2, core2)))
    return lax.ppermute(buf, ALL, pairs)


def rows_swap(inner, outer):
    return (
        swap(inner, lambda x, y, z, c: (x, y, z, 1 - c)),
        swap(outer, lambda x, y, z, c: (x + 2 * c - 1, y, z, 1 - c)),
    )


def cols_swap(inner, outer):
    return (
        swap(inner, lambda x, y, z, c: (x, y, z ^ 1, c)),
        swap(outer, lambda x, y, z, c: (x, y + 2 * ((z + y) % 2) - 1, z, c)),
    )


def ordered(first, later):
    got = lax.optimization_barrier((first[0],) + tuple(later))
    return [got[0]] + list(first[1:]), list(got[1:])


def call(body, outs, scratch=(), flops=0, size=3 << 20, name=None, **specs):
    return pl.pallas_call(
        body,
        out_shape=outs,
        scratch_shapes=list(scratch),
        compiler_params=pltpu.CompilerParams(vmem_limit_bytes=48 << 20),
        cost_estimate=pl.CostEstimate(flops=flops, bytes_accessed=size, transcendentals=0),
        name=name,
        **specs,
    )


def shaped(*dims, dtype=BF):
    return jax.ShapeDtypeStruct(dims, dtype)


DEALT = (2, 2, 4, 16, LANES)
FAR = pl.BlockSpec(memory_space=pltpu.HBM)
NEAR = pl.BlockSpec(memory_space=pltpu.VMEM)


def lanes_of(group):
    return pl.ds(pl.multiple_of(group * LANES, LANES), LANES)


def run_copies(pairs, sems):
    copies = [pltpu.make_async_copy(a, b, sems.at[n]) for n, (a, b) in enumerate(pairs)]
    for c in copies:
        c.start()
    for c in copies:
        c.wait()


def pack_body(*refs):
    ins, outs, sems = refs[:2], refs[2:-1], refs[-1]
    run_copies(
        [
            (ref.at[:, :, :, lanes_of(group)], out.at[i])
            for group, out in zip(groups_out(), outs)
            for i, ref in enumerate(ins)
        ],
        sems,
    )


def pack(a, b, name):
    return call(
        pack_body,
        [shaped(*DEALT)] * GROUPS,
        [pltpu.SemaphoreType.DMA((2 * GROUPS,))],
        in_specs=[FAR] * 2,
        out_specs=[NEAR] * GROUPS,
        name=name,
    )(a, b)


def unpack_body(*refs, turns, held):
    bufs, outs, sems = refs[: len(turns)], refs[len(turns) + held : -1], refs[-1]
    groups = groups_out()
    run_copies(
        [
            (buf.at[i], ref.at[:, :, :, lanes_of(groups[turn])])
            for turn, buf in zip(turns, bufs)
            for i, ref in enumerate(outs)
        ],
        sems,
    )


def unpack(bufs, name, turns=tuple(range(GROUPS)), into=()):
    return call(
        partial(unpack_body, turns=turns, held=len(into)),
        [shaped(2, 4, 16, GROUPS * LANES)] * 2,
        [pltpu.SemaphoreType.DMA((2 * len(turns),))],
        in_specs=[NEAR] * len(turns) + [FAR] * len(into),
        out_specs=[FAR] * 2,
        input_output_aliases={len(turns) + i: i for i in range(len(into))},
        name=name,
    )(*(bufs[t] for t in turns), *into)


def spot(src, t, h):
    return pl.ds(pl.multiple_of((src % 2) * 256 + (src // 2) * 32 + h * 64 + t * 16, 16), 16)


BLOCK = [(t, h) for t in range(2) for h in range(4)]


def gather_blocks(bufs, i, dest):
    for src, buf in zip(blocks_in(), bufs):
        for t, h in BLOCK:
            dest[i, spot(src, t, h), :] = buf[i, t, h]


def edge_pick(transpose, rows=8):
    few, many = 16 * rows, 64 * rows
    shape = (many, few) if transpose else (few, many)
    e = lax.broadcasted_iota(jnp.int32, shape, 1 if transpose else 0)
    token = lax.broadcasted_iota(jnp.int32, shape, 0 if transpose else 1)
    want = e % (8 * rows) // 2 * 16 + e % 2 + 14 * (e // (8 * rows))
    return jnp.where(token == want, 1.0, 0.0).astype(BF)


def side_slots(block):
    return 1 - block, block


def row_slots(half):
    return 1 - half, half


def at_16(start, size=16):
    return pl.ds(pl.multiple_of(start, 16), size)


def own_body(*refs):
    bufs, (own, *outs), edges = refs[:GROUPS], refs[GROUPS:-1], refs[-1]
    _, _, block, _ = place()
    pick = edge_pick(False)
    for i in range(2):
        gather_blocks(bufs, i, own)
        both = jnp.dot(pick, own[i], preferred_element_type=F32).astype(BF)
        edges[0, i] = both[:64]
        edges[1, i] = both[64:]
    for out, slot in zip(outs, side_slots(block)):
        out[...] = edges[slot]


def own_kv(bufs):
    outs = [shaped(2, 512, LANES), shaped(2, 64, LANES), shaped(2, 64, LANES)]
    return call(own_body, outs, [pltpu.VMEM((2, 2, 64, LANES), BF)], name="own_kv")(*bufs)


def rows_body(own, inner, outer, *outs):
    _, half, block, _ = place()
    for out, below in zip(outs, row_slots(half)):
        out[:, 0:128] = own[:, at_16(below * 384, 128)]
        for side, slot in zip((inner, outer), side_slots(block)):
            out[:, at_16(128 + slot * 16)] = side[:, at_16(below * 48)]


def rows_out(own, inner, outer):
    return call(rows_body, [shaped(2, 160, LANES)] * 2, name="rows_out")(own, inner, outer)


NT = (((1,), (1,)), ((), ()))
TN = (((0,), (0,)), ((), ()))


def row_sums(x):
    high = x.astype(BF)
    low = (x - high.astype(F32)).astype(BF)
    ones = jnp.ones((16, HEAD), BF)
    sums = lax.dot_general(ones, high, NT, preferred_element_type=F32)
    sums += lax.dot_general(ones, low, NT, preferred_element_type=F32)
    return sums[0:1]


def attend_body(window, own, col_in, col_out, row_in, row_out, *refs):
    qd = refs[:GROUPS]
    back = refs[GROUPS : 2 * GROUPS]
    own_grad, rows_grad, *cols_back = refs[2 * GROUPS : 2 * GROUPS + 4]
    kv_mid, kv_side, g_mid, g_side, q_all, o_all = refs[2 * GROUPS + 4 :]
    group, half, block, x = place()
    w_at = lax.axis_index("wa") // 2 * 2 + block
    w_last = lax.axis_size("wa") - 1
    scale = 1.0 / math.sqrt(HEAD)
    log2e = 1.0 / math.log(2.0)

    rows = list(zip((row_in, row_out), row_slots(half)))
    for i in range(2):
        kv_mid[i, 128:640] = own[i]
        for side, slot in zip((col_in, col_out), side_slots(block)):
            kv_side[slot, i, 16:80] = side[i]
        for buf, below in rows:
            kv_mid[i, at_16(below * 640, 128)] = buf[i, 0:128]
            for slot in range(2):
                kv_side[slot, i, at_16(below * 80)] = buf[i, 128 + 16 * slot : 144 + 16 * slot]
        gather_blocks(qd, i, q_all)

    qi = lax.broadcasted_iota(jnp.int32, (1, 128), 1)
    q_t, q_w = qi // 32 % 2, qi % 16 // 2
    ki = lax.broadcasted_iota(jnp.int32, (160, 1), 0)
    mid = ki < 128
    ks = jnp.where(ki < 144, ki - 128, ki - 144)
    k_t = jnp.where(mid, ki // 32 % 2, ks // 4 % 2)
    k_w = jnp.where(mid, ki % 16 // 2, jnp.where(ki < 144, -1, 8))
    beside = ((k_w >= 0) | (w_at > 0)) & ((k_w < 8) | (w_at < w_last))
    t_far, w_far = jnp.abs(q_t - k_t), jnp.where(beside, jnp.abs(q_w - k_w), 99)
    tile_row = (x * 2 + half) * 4 - 1
    tile_rows = 4 * 8

    for n in range(GH):
        f = slice(n * HEAD, (n + 1) * HEAD)
        head = group * GH + n
        rad_t, rad_h, rad_w = window[head, 0], window[head, 1], window[head, 2]
        base = jnp.where((t_far <= rad_t) & (w_far <= rad_w), 0.0, NEG)
        all_w, all_ds, held = [], [], []
        side_g = [[[None] * 6, [None] * 6], [[None] * 6, [None] * 6]]
        for blk in range(4):
            biases = []
            for j in range(3):
                row = tile_row + blk + j
                seen = (row >= 0) & (row < tile_rows) & (abs(j - 1) <= rad_h)
                biases.append(base + jnp.where(seen, 0.0, NEG))
            bias = jnp.concatenate(
                [biases[j][lo:hi] for lo, hi in ((0, 128), (128, 144), (144, 160)) for j in range(3)],
                axis=0,
            )
            mid_at, side_at, q_at = pl.ds(128 * blk, 384), pl.ds(16 * blk, 48), pl.ds(128 * blk, 128)
            k, v = (
                jnp.concatenate(
                    [kv_mid[i, mid_at, f], kv_side[0, i, side_at, f], kv_side[1, i, side_at, f]], axis=0
                )
                for i in range(2)
            )
            q, do = q_all[0, q_at, f], q_all[1, q_at, f]
            s = lax.dot_general(k, q, NT, preferred_element_type=F32)
            dp = lax.dot_general(v, do, NT, preferred_element_type=F32)
            held.append((k, v, q, do, s, dp, bias))
        soft = []
        for blk, (k, v, q, do, s, dp, bias) in enumerate(held):
            s = s * (scale * log2e) + bias
            e = jnp.exp2(s - jnp.max(s, axis=0, keepdims=True))
            p = e * (1.0 / jnp.sum(e, axis=0, keepdims=True))
            wts = p.astype(BF)
            o = lax.dot_general(wts, v, TN, preferred_element_type=F32).astype(BF)
            o_all[0, pl.ds(128 * blk, 128), f] = o
            soft.append((p, wts, row_sums(do.astype(F32) * o.astype(F32))))
        for blk, (k, v, q, do, s, dp, bias) in enumerate(held):
            p, wts, delta = soft[blk]
            ds = (p * (dp - delta)).astype(BF)
            dq = lax.dot_general(ds, k, TN, preferred_element_type=F32) * scale
            o_all[1, pl.ds(128 * blk, 128), f] = dq.astype(BF)
            all_ds.append(ds)
            all_w.append(wts)
            for i, (a, b) in enumerate(((ds, q), (wts, do))):
                part = jnp.dot(a[384:480], b, preferred_element_type=F32)
                for lr in range(2):
                    for o_ in range(3):
                        piece = part[48 * lr + 16 * o_ : 48 * lr + 16 * o_ + 16]
                        have = side_g[i][lr][blk + o_]
                        side_g[i][lr][blk + o_] = piece if have is None else have + piece
        for i, a in enumerate((all_ds, all_w)):
            mul = scale if i == 0 else 1.0
            for j in range(6):
                blks = [b for b in range(4) if 0 <= j - b <= 2]
                lhs = [a[b][128 * (j - b) : 128 * (j - b) + 128] for b in blks]
                lhs = lhs[0] if len(lhs) == 1 else jnp.concatenate(lhs, axis=1)
                rhs = q_all[i, pl.ds(128 * blks[0], 128 * len(blks)), f]
                g_mid[i, 128 * j : 128 * j + 128, f] = (
                    jnp.dot(lhs, rhs, preferred_element_type=F32) * mul
                )
                for slot in range(2):
                    g_side[slot, i, 16 * j : 16 * j + 16, f] = side_g[i][slot][j] * mul

    for src, out in zip(blocks_in(), back):
        for i in range(2):
            for t, h in BLOCK:
                out[i, t, h] = o_all[i, spot(src, t, h), :]
    for i in range(2):
        own_grad[i] = g_mid[i, 128:640]
        for n, (_, below) in enumerate(rows):
            rows_grad[n, i] = g_mid[i, at_16(below * 640, 128)]
        for out, slot in zip(cols_back, side_slots(block)):
            out[i] = g_side[slot, i].astype(BF)


def attend(window, own, cols, rows, qd):
    outs = [shaped(*DEALT)] * GROUPS + [
        shaped(2, 512, LANES, dtype=F32),
        shaped(2, 2, 128, LANES, dtype=F32),
        shaped(2, 96, LANES),
        shaped(2, 96, LANES),
    ]
    ins = [own, *cols, *rows, *qd]
    scratch = [
        pltpu.VMEM((2, 768, LANES), BF),
        pltpu.VMEM((2, 2, 96, LANES), BF),
        pltpu.VMEM((2, 768, LANES), F32),
        pltpu.VMEM((2, 2, 96, LANES), F32),
        pltpu.VMEM((2, 512, LANES), BF),
        pltpu.VMEM((2, 512, LANES), BF),
    ]
    return call(
        attend_body,
        outs,
        scratch,
        in_specs=[pl.BlockSpec(memory_space=pltpu.SMEM)] + [NEAR] * len(ins),
        out_specs=[NEAR] * len(outs),
        flops=1200000000,
        size=8 << 20,
        name="attend",
    )(window, *ins)


def rows_back_body(rows_grad, col_in, col_out, *refs):
    outs, edges = refs[:2], refs[2]
    _, half, block, _ = place()
    spread = edge_pick(True, 2)
    for side, slot in zip((col_in, col_out), side_slots(block)):
        edges[slot] = side[...]
    for n, (out, below) in enumerate(zip(outs, row_slots(half))):
        for i in range(2):
            both = jnp.concatenate([edges[slot, i, at_16(below * 80)] for slot in range(2)], axis=0)
            total = rows_grad[n, i] + jnp.dot(spread, both, preferred_element_type=F32)
            out[i] = total.astype(BF)


def rows_back(rows_grad, cols):
    scratch = [pltpu.VMEM((2, 2, 96, LANES), BF)]
    return call(rows_back_body, [shaped(2, 128, LANES)] * 2, scratch, name="rows_back")(rows_grad, *cols)


def final_body(own_grad, row_in, row_out, col_in, col_out, *refs):
    outs, (total, edges) = refs[:GROUPS], refs[GROUPS:]
    _, half, block, _ = place()
    spread = edge_pick(True)
    for side, slot in zip((col_in, col_out), side_slots(block)):
        edges[slot] = side[:, 16:80]
    for i in range(2):
        both = jnp.concatenate([edges[0, i], edges[1, i]], axis=0)
        total[i] = own_grad[i] + jnp.dot(spread, both, preferred_element_type=F32)
        for buf, below in zip((row_in, row_out), row_slots(half)):
            total[i, at_16(below * 384, 128), :] += buf[i].astype(F32)
        for src, out in zip(blocks_in(), outs):
            for t, h in BLOCK:
                out[i, t, h] = total[i, spot(src, t, h), :].astype(BF)


def final(own_grad, rows, cols):
    scratch = [pltpu.VMEM((2, 512, LANES), F32), pltpu.VMEM((2, 2, 64, LANES), BF)]
    return call(final_body, [shaped(*DEALT)] * GROUPS, scratch, name="final")(own_grad, *rows, *cols)


def local(queries, keys, values, out_grad, head_window):
    queries, keys, values, out_grad = (
        pltpu.with_memory_space_constraint(v, pltpu.HBM) for v in (queries, keys, values, out_grad)
    )
    sent = list(pack(keys, values, "pack_kv"))
    sent, (queries, out_grad) = ordered(sent, (queries, out_grad))
    kv = deal(sent, False)
    ask = list(pack(queries, out_grad, "pack_qd"))
    qd = deal(ask, False)
    kv, qd[:1] = ordered(kv, qd[:1])
    own, *edges = own_kv(kv)
    cols = cols_swap(*edges)
    cols, qd[1:] = ordered(cols, qd[1:])
    rows = rows_swap(*rows_out(own, *cols))
    results = attend(head_window, own, cols, rows, qd)
    oq = deal(results[:GROUPS], True)
    own_grad, rows_grad, *cols_back = results[GROUPS:]
    cols = cols_swap(*cols_back)
    rows = rows_swap(*rows_back(rows_grad, cols))
    rows, oq[0:2] = ordered(rows, oq[0:2])
    dkv = deal(final(own_grad, rows, cols), True)
    attended, query_grad = unpack(oq, "unpack_oq")
    early = unpack(dkv, "unpack_dkv_early", (0, 1, 2))
    key_grad, value_grad = unpack(dkv, "unpack_dkv_last", (3,), early)
    return attended, query_grad, key_grad, value_grad


def solution(mesh):
    spec = P("ta", "ha", "wa", None)
    return jax.shard_map(
        local,
        mesh=mesh,
        in_specs=(spec,) * 4 + (P(),),
        out_specs=(spec,) * 4,
        check_vma=False,
    )
```
